32 devices in a mesh: col: 8 (over z, x), row: 4 (over y, core).
Axes of the slice: x: 2, y: 2, z: 4, core: 2. Of those that a mesh axis runs over, the one named last changes fastest.
Arguments:
- amp_owned: bfloat16 [9216, 4096], P(('col', 'row')), may hold values from -6 to 6
- pair_of_slot: int32 [9216], replicated, may hold values from 0 to 9215, as said below
- amp_tiles: int32 [72, 32], replicated, may hold values 0 or 1
- integrals: bfloat16 [2, 2048, 8192], P(None, 'row', 'col'), may hold values from -0.09375 to 0.09375
- integral_tile_mask: int32 [2, 16, 64], replicated, may hold values 0 or 1
Outputs:
- ladder: float32 [9216, 8192], P('row', 'col')
The draws below stay inside these ranges and needn't reach their ends.
Inputs may be any that keep to these rules, and one draw needn't show every extreme that they name: `pair_of_slot`: a permutation of the 9216 occupied pairs; owner slot q lies on the device of index q // 288 along col+row; one owner holds at most 144 pairs of any one grid row (pairs r * 9216 / 4 to (r + 1) * 9216 / 4 - 1), and some owner holds exactly 144 of each grid row.
All inputs are finite; a program needn't handle non-finite values.
Results may differ from the reference program's by a relative error of at most 0.0003.
Values may be sent and summed in bfloat16 or wider, within the bound.
A program may use at most 128 MiB of HBM per device.

```python
import jax
import jax.numpy as jnp

M = 9216
TILE_EDGE = 128
SECTIONS = 2
CONTRACTED_PAIRS = 2048
NC = 1024
N = 8192
N_COL = 8
N_ROW = 4


def draw_pair_of_slot(key, part):
    devices = N_COL * N_ROW
    own_rows = M // devices
    unit_count = own_rows // N_ROW
    grid_rows = M // N_ROW
    half_rows = N_ROW // 2
    blocks = devices // N_ROW
    key_extra, key_order, key_offset, key_rows, key_slots = jax.random.split(key, 5)
    extra = jax.random.randint(key_extra, (blocks, half_rows), 0, unit_count + 1)
    extra = extra.at[:, 0].set(unit_count)
    profile = jnp.concatenate([unit_count + extra, unit_count - extra[:, ::-1]], axis=1)
    orders = jax.vmap(lambda sub_key: jax.random.permutation(sub_key, N_ROW))(jax.random.split(key_order, blocks))
    profile = jnp.take_along_axis(profile, orders, axis=1)
    offsets = jax.random.randint(key_offset, (blocks,), 0, N_ROW)
    member = jnp.arange(N_ROW)
    where_in = (member[None, None, :] - member[None, :, None] - offsets[:, None, None]) % N_ROW
    counts = jnp.take_along_axis(jnp.broadcast_to(profile[:, None, :], (blocks, N_ROW, N_ROW)), where_in, axis=2)
    counts = counts.reshape(devices, N_ROW)
    grid_start = jnp.cumsum(counts, axis=0) - counts
    slot_end = jnp.cumsum(counts, axis=1)
    slot_start = slot_end - counts
    slots = jnp.arange(own_rows)
    which_row = jnp.sum((slot_end[:, None, :] <= slots[None, :, None]).astype(jnp.int32), axis=2)
    which_row = jnp.minimum(which_row, N_ROW - 1)
    within = slots[None, :] - jnp.take_along_axis(slot_start, which_row, axis=1)
    position = jnp.take_along_axis(grid_start, which_row, axis=1) + within
    row_perms = jax.vmap(lambda sub_key: jax.random.permutation(sub_key, grid_rows))(jax.random.split(key_rows, N_ROW))
    global_rows = which_row * grid_rows + row_perms[which_row, position]
    shuffles = jax.vmap(lambda sub_key: jax.random.permutation(sub_key, own_rows))(jax.random.split(key_slots, devices))
    global_rows = jnp.take_along_axis(global_rows, shuffles, axis=1)
    return global_rows.reshape(M).astype(jnp.int32)


def place_ends(entries, rng, smallest, high):
    dims = entries.shape
    spot = [jax.random.randint(jax.random.fold_in(rng, axis), (), 0, dims[axis]) for axis in range(len(dims))]
    entries = entries.at[tuple(spot)].set(smallest)
    longest = dims.index(max(dims))
    spot[longest] = (spot[longest] + 1) % dims[longest]
    return entries.at[tuple(spot)].set(high)


def steps_of(own_key, dims, pieces, low, high):
    gain, own = 1.0, jax.random.fold_in(own_key, 6)
    for axis_at, blocks in pieces:
        steps = jnp.exp(jax.random.uniform(jax.random.fold_in(own, axis_at), (blocks,), jnp.float32, low / len(pieces), high / len(pieces)))
        gain = gain * jnp.repeat(steps, dims[axis_at] // blocks).reshape([-1 if axis == axis_at else 1 for axis in range(len(dims))])
    return gain


def noise(key, shape, deviation, most, cuts=(), kind=jnp.bfloat16):
    gain = steps_of(key, shape, cuts, -0.22, 0.18) if cuts else 1.0
    values = jax.random.normal(key, shape, jnp.float32) * deviation * gain
    return jnp.minimum(jnp.maximum(values, -most), most).astype(kind)


def setup_inputs(seed: int = 0) -> dict:
    arg_keys = jax.random.split(jax.random.key(seed), 6)
    amp_owned = noise(arg_keys[0], (M, SECTIONS * CONTRACTED_PAIRS), 1.0, 6.0, ((0, 32),))
    pair_of_slot = draw_pair_of_slot(jax.random.fold_in(arg_keys[5], 71), 0)
    amp_tiles = place_ends((jax.random.randint(arg_keys[2], (M // TILE_EDGE, SECTIONS * CONTRACTED_PAIRS // TILE_EDGE), 0, 3) < 2).astype(jnp.int32), jax.random.fold_in(arg_keys[2], 1), 0, 1)
    integrals = noise(arg_keys[3], (SECTIONS, CONTRACTED_PAIRS, N), (SECTIONS * CONTRACTED_PAIRS) ** -0.5, 0.09375, ((1, 4), (2, 8)))
    integral_tile_mask = place_ends((jax.random.randint(arg_keys[4], (SECTIONS, CONTRACTED_PAIRS // TILE_EDGE, N // TILE_EDGE), 0, 3) < 2).astype(jnp.int32), jax.random.fold_in(arg_keys[4], 1), 0, 1)
    return dict(amp_owned=amp_owned, pair_of_slot=pair_of_slot, amp_tiles=amp_tiles, integrals=integrals, integral_tile_mask=integral_tile_mask)


def apply_tile_blocks(block_data, tile_map, tile_size):
    row_count, col_count = block_data.shape
    shaped = block_data.reshape(row_count // tile_size, tile_size, col_count // tile_size, tile_size)
    shaped = shaped * tile_map.astype(block_data.dtype)[:, None, :, None]
    return shaped.reshape(row_count, col_count)


def reference(amp_owned, pair_of_slot, amp_tiles, integrals, integral_tile_mask):
    amplitude_complete = jnp.zeros((M, SECTIONS * CONTRACTED_PAIRS), jnp.bfloat16).at[pair_of_slot].set(amp_owned)
    amplitude_complete = apply_tile_blocks(amplitude_complete, amp_tiles, TILE_EDGE)
    ladder = jnp.zeros((M, NC * N_COL), jnp.float32)
    for section_part in range(SECTIONS):
        virtual_integrals = apply_tile_blocks(integrals[section_part], integral_tile_mask[section_part], TILE_EDGE)
        ladder = ladder + jnp.dot(amplitude_complete[:, section_part * CONTRACTED_PAIRS:(section_part + 1) * CONTRACTED_PAIRS], virtual_integrals, preferred_element_type=jnp.float32)
    return 0.5 * ladder
```

```python
import functools

import jax
import jax.numpy as jnp
from jax import lax
from jax.experimental import pallas as pl
from jax.experimental.pallas import tpu as pltpu
from jax.sharding import PartitionSpec as P

MESH = pl.DeviceIdType.MESH


def apply_tile_blocks(block_data, tile_map, tile_size):
    row_count, col_count = block_data.shape
    shaped = block_data.reshape(
        row_count // tile_size, tile_size, col_count // tile_size, tile_size
    )
    shaped = shaped * tile_map.astype(block_data.dtype)[:, None, :, None]
    return shaped.reshape(row_count, col_count)


def spread_kernel(
    lines, width, chunk, a_ref, b_ref, o_ref, full, load, zsend, zrecv, xsend, xrecv
):
    col = lax.axis_index("col")
    z, x = col // width, col % width
    rows = a_ref.shape[0]
    chunks = rows // chunk
    out_cols = o_ref.shape[1]

    barrier = pltpu.get_barrier_semaphore()
    for side in (1, -1):
        near = z + side

        @pl.when((near >= 0) & (near < lines))
        def _(near=near):
            pl.semaphore_signal(
                barrier, inc=1, device_id={"col": near * width + x}, device_id_type=MESH
            )

    for e in range(1, width):
        pl.semaphore_signal(
            barrier, inc=1, device_id={"col": z * width + (x + e) % width}, device_id_type=MESH
        )
    ends = (z == 0).astype(jnp.int32) + (z == lines - 1).astype(jnp.int32)
    pl.semaphore_wait(barrier, width + 1 - ends)

    def along(origin, j, side):
        piece = full.at[origin * width + x, pl.ds(pl.multiple_of(j * chunk, chunk), chunk)]
        return pltpu.make_async_remote_copy(
            src_ref=piece,
            dst_ref=piece,
            send_sem=zsend.at[0 if side > 0 else 1, origin, j],
            recv_sem=zrecv.at[origin, j],
            device_id={"col": (z + side) * width + x},
            device_id_type=MESH,
        )

    def across(origin, j, e, which=None):
        held = x if which is None else which
        piece = full.at[origin * width + held, pl.ds(pl.multiple_of(j * chunk, chunk), chunk)]
        return pltpu.make_async_remote_copy(
            src_ref=piece,
            dst_ref=piece,
            send_sem=xsend.at[e - 1, origin, j],
            recv_sem=xrecv.at[origin * width + held, j],
            device_id={"col": z * width + (x + e) % width},
            device_id_type=MESH,
        )

    def multiply(k, j, first=False):
        at = pl.ds(pl.multiple_of(j * chunk, chunk), chunk)

        def part(n, carry):
            cols = pl.ds(pl.multiple_of(n * 512, 512), 512)
            term = 0.5 * jnp.dot(
                full[k, at, :], b_ref[k, :, cols], preferred_element_type=jnp.float32
            )
            if first:
                o_ref[at, cols] = term
            else:
                o_ref[at, cols] += term
            return carry

        lax.fori_loop(0, out_cols // 512, part, 0)

    own = pltpu.make_async_copy(a_ref, full.at[col], load)
    own.start()
    own.wait()

    def step(t, carry):
        d, j = t // chunks, t % chunks

        @pl.when(d == 0)
        def _():
            for side in (1, -1):

                @pl.when((z + side >= 0) & (z + side < lines))
                def _(side=side):
                    along(z, j, side).start()

            for e in range(1, width):
                across(z, j, e).start()
            multiply(col, j, True)

        for side in (1, -1):
            origin = z - side * d

            @pl.when((d > 0) & (d < lines) & (origin >= 0) & (origin < lines))
            def _(side=side, origin=origin):
                along(origin, j, -side).wait_recv()

                @pl.when((z + side >= 0) & (z + side < lines))
                def _():
                    along(origin, j, side).start()

                for e in range(1, width):
                    across(origin, j, e).start()
                multiply(origin * width + x, j)

        for side in (1, -1):
            origin = z - side * (d - 1)
            due = (d > 0) if side > 0 else (d > 1)

            @pl.when(due & (origin >= 0) & (origin < lines))
            def _(origin=origin):
                for e in range(1, width):
                    there = (x + e) % width
                    across(origin, j, e, there).wait_recv()
                    multiply(origin * width + there, j)

        return carry

    lax.fori_loop(0, (lines + 1) * chunks, step, 0)

    def drain(t, carry):
        origin, j = t // chunks, t % chunks

        @pl.when((origin <= z) & (z < lines - 1))
        def _():
            along(origin, j, 1).wait_send()

        @pl.when((origin >= z) & (z > 0))
        def _():
            along(origin, j, -1).wait_send()

        for e in range(1, width):
            across(origin, j, e).wait_send()
        return carry

    lax.fori_loop(0, lines * chunks, drain, 0)


def spread_multiply(amp_piece, vint, n_col):
    lines = 4 if n_col % 4 == 0 else n_col
    width = n_col // lines
    rows, depth = amp_piece.shape
    out_cols = vint.shape[2]
    chunk = 384 if rows % 384 == 0 else rows
    chunks = rows // chunk
    return pl.pallas_call(
        functools.partial(spread_kernel, lines, width, chunk),
        out_shape=jax.ShapeDtypeStruct((rows, out_cols), jnp.float32),
        in_specs=[
            pl.BlockSpec(memory_space=pl.ANY),
            pl.BlockSpec(memory_space=pltpu.VMEM),
        ],
        out_specs=pl.BlockSpec(memory_space=pltpu.VMEM),
        scratch_shapes=[
            pltpu.VMEM((n_col, rows, depth), jnp.bfloat16),
            pltpu.SemaphoreType.DMA,
            pltpu.SemaphoreType.DMA((2, lines, chunks)),
            pltpu.SemaphoreType.DMA((lines, chunks)),
            pltpu.SemaphoreType.DMA((max(width - 1, 1), lines, chunks)),
            pltpu.SemaphoreType.DMA((n_col, chunks)),
        ],
        compiler_params=pltpu.CompilerParams(
            collective_id=0, has_side_effects=True, vmem_limit_bytes=58 * 1024 * 1024
        ),
        cost_estimate=pl.CostEstimate(
            flops=2 * rows * depth * n_col * out_cols, bytes_accessed=40_000_000, transcendentals=0
        ),
    )(amp_piece, vint)


def on_device(amp_owned, pair_of_slot, amp_tiles, integrals, integral_tile_mask):
    n_col = lax.axis_size("col")
    n_row = lax.axis_size("row")
    col_at = lax.axis_index("col")
    row_at = lax.axis_index("row")
    own_rows, width_all = amp_owned.shape
    total_rows = pair_of_slot.shape[0]
    grid_rows = total_rows // n_row
    sections, slab_rows, out_cols = integrals.shape
    tile_size = total_rows // amp_tiles.shape[0]
    piece_cols = width_all // n_col
    row_tiles = grid_rows // tile_size
    piece_tiles = piece_cols // tile_size

    local_tile_rows = slab_rows // tile_size
    col_tiles = out_cols // tile_size
    tiles_int = lax.dynamic_slice(
        integral_tile_mask,
        (0, row_at * local_tile_rows, col_at * col_tiles),
        (sections, local_tile_rows, col_tiles),
    )
    masked = apply_tile_blocks(
        integrals.reshape(sections * slab_rows, out_cols),
        tiles_int.reshape(sections * local_tile_rows, col_tiles),
        tile_size,
    ).reshape(sections, slab_rows, out_cols)
    vint = lax.all_gather(masked, "row", axis=1, tiled=True)
    vint = vint.reshape(n_col, piece_cols, out_cols)

    dealt = amp_owned.reshape(own_rows, n_col, piece_cols).transpose(1, 0, 2)
    dealt = lax.all_to_all(dealt, "col", split_axis=0, concat_axis=0, tiled=True)
    everyone = lax.all_gather(dealt, "row", axis=0, tiled=False)
    everyone = everyone.reshape(total_rows, piece_cols)

    slot = jnp.arange(total_rows, dtype=jnp.int32)
    owner, within = slot // own_rows, slot % own_rows
    place = ((owner % n_row) * n_col + owner // n_row) * own_rows + within
    high = (
        (pair_of_slot // tile_size - row_at * row_tiles)[:, None]
        == jnp.arange(row_tiles, dtype=jnp.int32)[None, :]
    ).astype(jnp.bfloat16)
    low = (pair_of_slot % tile_size)[:, None] == jnp.arange(tile_size, dtype=jnp.int32)[None, :]
    zero = jnp.zeros((), jnp.bfloat16)
    low = jnp.concatenate(
        [
            jnp.where(low, (place // 128).astype(jnp.bfloat16)[:, None], zero),
            jnp.where(low, (place % 128).astype(jnp.bfloat16)[:, None], zero),
        ],
        axis=1,
    )
    found = lax.dot_general(
        high, low, (((0,), (0,)), ((), ())), preferred_element_type=jnp.float32
    ).astype(jnp.int32)
    found = (found[:, :tile_size] * 128 + found[:, tile_size:]).reshape(grid_rows)

    my_tiles = lax.dynamic_slice(
        amp_tiles, (row_at * row_tiles, col_at * piece_tiles), (row_tiles, piece_tiles)
    )
    amp_piece = apply_tile_blocks(
        everyone.at[found].get(mode="promise_in_bounds"), my_tiles, tile_size
    )
    return spread_multiply(amp_piece, vint, n_col)


def solution(mesh):
    placed = (P(("col", "row"), None), P(), P(), P(None, "row", "col"), P())
    return jax.shard_map(
        on_device, mesh=mesh, in_specs=placed, out_specs=P("row", "col"), check_vma=False
    )
```

```python
import functools

import jax
import jax.numpy as jnp
from jax import lax
from jax.experimental import pallas as pl
from jax.experimental.pallas import tpu as pltpu
from jax.sharding import PartitionSpec as P

MESH = pl.DeviceIdType.MESH


def apply_tile_blocks(block_data, tile_map, tile_size):
    row_count, col_count = block_data.shape
    shaped = block_data.reshape(
        row_count // tile_size, tile_size, col_count // tile_size, tile_size
    )
    shaped = shaped * tile_map.astype(block_data.dtype)[:, None, :, None]
    return shaped.reshape(row_count, col_count)


def spread_kernel(
    lines,
    width,
    n_row,
    chunk,
    tile,
    a_ref,
    i_ref,
    m_ref,
    o_ref,
    full,
    b_ref,
    load,
    zsend,
    zrecv,
    xsend,
    xrecv,
    bsend,
    bcore,
    brecv,
):
    col = lax.axis_index("col")
    row = lax.axis_index("row")
    planes = n_row // 2
    sections, slab_rows, _ = i_ref.shape
    core = row % 2
    partner = row + 1 - 2 * core
    z, x = col // width, col % width
    rows = a_ref.shape[0]
    chunks = rows // chunk
    out_cols = o_ref.shape[1]

    barrier = pltpu.get_barrier_semaphore()
    for side in (1, -1):
        near = z + side

        @pl.when((near >= 0) & (near < lines))
        def _(near=near):
            pl.semaphore_signal(
                barrier, inc=1, device_id={"col": near * width + x}, device_id_type=MESH
            )

    for e in range(1, width):
        pl.semaphore_signal(
            barrier, inc=1, device_id={"col": z * width + (x + e) % width}, device_id_type=MESH
        )
    pl.semaphore_signal(barrier, inc=1, device_id={"row": partner}, device_id_type=MESH)
    for e in range(1, planes):
        pl.semaphore_signal(
            barrier, inc=1, device_id={"row": (row + 2 * e) % n_row}, device_id_type=MESH
        )

    own = pltpu.make_async_copy(a_ref, full.at[col], load)
    own.start()
    tiles = slab_rows // tile
    for s in range(sections):
        for i in range(tiles):
            at = slice(i * tile, (i + 1) * tile)
            b_ref[s * n_row + row, at, :] = (
                i_ref[s, at, :] * m_ref[s * tiles + i : s * tiles + i + 1, :]
            )
    ends = (z == 0).astype(jnp.int32) + (z == lines - 1).astype(jnp.int32)
    pl.semaphore_wait(barrier, width + 1 - ends + planes)
    own.wait()

    def sent(s, held, to, sem):
        k = s * n_row + held
        return pltpu.make_async_remote_copy(
            src_ref=b_ref.at[k],
            dst_ref=b_ref.at[k],
            send_sem=sem,
            recv_sem=brecv.at[k],
            device_id={"row": to},
            device_id_type=MESH,
        )

    def beside(s, e):
        return sent(s, row, (row + 2 * e) % n_row, bsend.at[e - 1, s])

    def inside(s, e):
        held = (row + 2 * e) % n_row
        return sent(s, held, partner, bcore.at[e, s])

    def arrival(s, held):
        return sent(s, held, partner, bcore.at[0, s])

    def along(origin, j, side):
        piece = full.at[origin * width + x, pl.ds(pl.multiple_of(j * chunk, chunk), chunk)]
        return pltpu.make_async_remote_copy(
            src_ref=piece,
            dst_ref=piece,
            send_sem=zsend.at[0 if side > 0 else 1, origin, j],
            recv_sem=zrecv.at[origin, j],
            device_id={"col": (z + side) * width + x},
            device_id_type=MESH,
        )

    def across(origin, j, e, which=None):
        held = x if which is None else which
        piece = full.at[origin * width + held, pl.ds(pl.multiple_of(j * chunk, chunk), chunk)]
        return pltpu.make_async_remote_copy(
            src_ref=piece,
            dst_ref=piece,
            send_sem=xsend.at[e - 1, origin, j],
            recv_sem=xrecv.at[origin * width + held, j],
            device_id={"col": z * width + (x + e) % width},
            device_id_type=MESH,
        )

    def multiply(k, j, first=False):
        at = pl.ds(pl.multiple_of(j * chunk, chunk), chunk)

        def part(n, carry):
            cols = pl.ds(pl.multiple_of(n * 512, 512), 512)
            term = 0.5 * jnp.dot(
                full[k, at, :], b_ref[k, :, cols], preferred_element_type=jnp.float32
            )
            if first:
                o_ref[at, cols] = term
            else:
                o_ref[at, cols] += term
            return carry

        lax.fori_loop(0, out_cols // 512, part, 0)

    def step(t, carry):
        d, j = t // chunks, t % chunks

        @pl.when(d == 0)
        def _():
            for side in (1, -1):

                @pl.when((z + side >= 0) & (z + side < lines))
                def _(side=side):
                    along(z, j, side).start()

            for e in range(1, width):
                across(z, j, e).start()

        for s in range(sections):

            @pl.when(t == s)
            def _(s=s):
                for e in range(1, planes):
                    beside(s, e).start()
                inside(s, 0).start()

        for side in (1, -1):
            origin = z - side * d

            @pl.when((d > 0) & (d < lines) & (origin >= 0) & (origin < lines))
            def _(side=side, origin=origin):
                along(origin, j, -side).wait_recv()

                @pl.when((z + side >= 0) & (z + side < lines))
                def _():
                    along(origin, j, side).start()

                for e in range(1, width):
                    across(origin, j, e).start()

        for s in range(sections):

            @pl.when(t == chunks + (s + 1) * chunks // sections - 1)
            def _(s=s):
                for e in range(1, planes):
                    arrival(s, (row + 2 * e) % n_row).wait_recv()
                    inside(s, e).start()

        @pl.when(t == 2 * chunks)
        def _():
            for s in range(sections):
                for e in range(planes):
                    arrival(s, (partner + 2 * e) % n_row).wait_recv()

        @pl.when(d == 2)
        def _():
            multiply(col, j, True)

        def lagged(apart):
            for side in (1, -1):
                origin = z - side * apart

                @pl.when((apart < lines) & (origin >= 0) & (origin < lines))
                def _(origin=origin):
                    multiply(origin * width + x, j)

        def crossed(apart):
            for side in (1, -1):
                origin = z - side * apart
                due = True if side > 0 else apart > 0

                @pl.when(due & (origin >= 0) & (origin < lines))
                def _(origin=origin):
                    for e in range(1, width):
                        there = (x + e) % width
                        across(origin, j, e, there).wait_recv()
                        multiply(origin * width + there, j)

        def late(i, carry):
            lagged(i)
            crossed(i - 1)
            return carry

        lax.fori_loop(jnp.where(d == 2, 1, d), jnp.where(d < 2, d, d + 1), late, 0)
        return carry

    lax.fori_loop(0, (lines + 1) * chunks, step, 0)

    def drain(t, carry):
        origin, j = t // chunks, t % chunks

        @pl.when((origin <= z) & (z < lines - 1))
        def _():
            along(origin, j, 1).wait_send()

        @pl.when((origin >= z) & (z > 0))
        def _():
            along(origin, j, -1).wait_send()

        for e in range(1, width):
            across(origin, j, e).wait_send()
        return carry

    lax.fori_loop(0, lines * chunks, drain, 0)
    for s in range(sections):
        for e in range(1, planes):
            beside(s, e).wait_send()
        for e in range(planes):
            inside(s, e).wait_send()


def spread_multiply(amp_piece, integrals, factors, n_col, n_row, tile):
    lines = 4 if n_col % 4 == 0 else n_col
    width = n_col // lines
    rows, depth = amp_piece.shape
    sections, slab_rows, out_cols = integrals.shape
    planes = n_row // 2
    chunk = 384 if rows % 384 == 0 else rows
    chunks = rows // chunk
    return pl.pallas_call(
        functools.partial(spread_kernel, lines, width, n_row, chunk, tile),
        out_shape=jax.ShapeDtypeStruct((rows, out_cols), jnp.float32),
        in_specs=[
            pl.BlockSpec(memory_space=pl.ANY),
            pl.BlockSpec(memory_space=pltpu.VMEM),
            pl.BlockSpec(memory_space=pltpu.VMEM),
        ],
        out_specs=pl.BlockSpec(memory_space=pltpu.VMEM),
        scratch_shapes=[
            pltpu.VMEM((n_col, rows, depth), jnp.bfloat16),
            pltpu.VMEM((sections * n_row, slab_rows, out_cols), jnp.bfloat16),
            pltpu.SemaphoreType.DMA,
            pltpu.SemaphoreType.DMA((2, lines, chunks)),
            pltpu.SemaphoreType.DMA((lines, chunks)),
            pltpu.SemaphoreType.DMA((max(width - 1, 1), lines, chunks)),
            pltpu.SemaphoreType.DMA((n_col, chunks)),
            pltpu.SemaphoreType.DMA((max(planes - 1, 1), sections)),
            pltpu.SemaphoreType.DMA((planes, sections)),
            pltpu.SemaphoreType.DMA((sections * n_row,)),
        ],
        compiler_params=pltpu.CompilerParams(
            collective_id=0, has_side_effects=True, vmem_limit_bytes=58 * 1024 * 1024
        ),
        cost_estimate=pl.CostEstimate(
            flops=2 * rows * depth * n_col * out_cols, bytes_accessed=40_000_000, transcendentals=0
        ),
    )(amp_piece, integrals, factors)


def deal_kernel(
    n_row, n_col, tile, a_ref, pair_ref, place_ref, out_ref, found_ref, keep, asend, ysend, csend, recv
):
    col = lax.axis_index("col")
    row = lax.axis_index("row")
    planes = n_row // 2
    partner = row + 1 - 2 * (row % 2)
    _, _, own_rows, width = out_ref.shape

    barrier = pltpu.get_barrier_semaphore()
    for e in range(1, n_col):
        pl.semaphore_signal(
            barrier, inc=1, device_id={"col": (col + e) % n_col}, device_id_type=MESH
        )
    pl.semaphore_signal(barrier, inc=1, device_id={"row": partner}, device_id_type=MESH)
    for e in range(1, planes):
        pl.semaphore_signal(
            barrier, inc=1, device_id={"row": (row + 2 * e) % n_row}, device_id_type=MESH
        )
    pl.semaphore_wait(barrier, n_col + planes - 1)

    def cut(c):
        return a_ref.at[:, pl.ds(pl.multiple_of(c * width, width), width)]

    def dealt(e):
        to = (col + e) % n_col
        return pltpu.make_async_remote_copy(
            src_ref=cut(to),
            dst_ref=out_ref.at[row, col],
            send_sem=asend.at[e],
            recv_sem=recv.at[row, col],
            device_id={"col": to},
            device_id_type=MESH,
        )

    def sent(held, c, to, sem, src=None):
        return pltpu.make_async_remote_copy(
            src_ref=out_ref.at[held, c] if src is None else src,
            dst_ref=out_ref.at[held, c],
            send_sem=sem,
            recv_sem=recv.at[held, c],
            device_id={"row": to},
            device_id_type=MESH,
        )

    def beside(c, e, src=None):
        return sent(row, c, (row + 2 * e) % n_row, ysend.at[e - 1, c], src)

    def inside(c, e, src=None):
        return sent((row + 2 * e) % n_row, c, partner, csend.at[e, c], src)

    mine = pltpu.make_async_copy(cut(col), out_ref.at[row, col], keep)
    mine.start()
    for e in range(1, planes):
        beside(col, e, cut(col)).start()

    def start(e, carry):
        dealt(e).start()
        return carry

    lax.fori_loop(1, n_col, start, 0)
    inside(col, 0, cut(col)).start()

    total = pair_ref.shape[1]
    tiles = found_ref.shape[0]
    block = total // 8
    found_ref[...] = jnp.zeros_like(found_ref)

    def invert(i, carry):
        at = pl.ds(pl.multiple_of(i * block, block), block)
        pairs = pair_ref[:, at]
        here = lax.broadcasted_iota(jnp.int32, (tiles, block), 0) * tile + row * (tiles * tile)
        high = jnp.where((pairs >= here) & (pairs < here + tile), 1.0, 0.0).astype(jnp.bfloat16)
        low = (pairs & (tile - 1)) == lax.broadcasted_iota(jnp.int32, (tile, block), 0)
        for half in range(2):
            value = jnp.where(low, place_ref[half : half + 1, at], 0.0).astype(jnp.bfloat16)
            found_ref[:, half * tile : (half + 1) * tile] += lax.dot_general(
                high, value, (((1,), (1,)), ((), ())), preferred_element_type=jnp.float32
            )
        return carry

    lax.fori_loop(0, 8, invert, 0)

    def step(e, carry):
        @pl.when((e > 0) & (e < n_col))
        def _():
            c = (col + n_col - e) % n_col
            sent(row, c, partner, csend.at[0, c]).wait_recv()
            for f in range(1, planes):
                beside(c, f).start()
            inside(c, 0).start()

        @pl.when(e > 0)
        def _():
            c = (col + n_col - (e - 1)) % n_col
            for f in range(1, planes):
                sent((row + 2 * f) % n_row, c, partner, csend.at[f, c]).wait_recv()
                inside(c, f).start()

        return carry

    lax.fori_loop(0, n_col + 1, step, 0)
    mine.wait()

    def drain(c, carry):
        for f in range(planes):
            sent((partner + 2 * f) % n_row, c, partner, csend.at[f, c]).wait_recv()
            inside(c, f).wait_send()
        for f in range(1, planes):
            beside(c, f).wait_send()

        @pl.when(c > 0)
        def _():
            dealt(c).wait_send()

        return carry

    lax.fori_loop(0, n_col, drain, 0)


def deal(amp_owned, pairs, places, n_row, n_col, tile):
    own_rows, width_all = amp_owned.shape
    tiles = pairs.shape[1] // n_row // tile
    planes = n_row // 2
    return pl.pallas_call(
        functools.partial(deal_kernel, n_row, n_col, tile),
        out_shape=(
            jax.ShapeDtypeStruct((n_row, n_col, own_rows, width_all // n_col), jnp.bfloat16),
            jax.ShapeDtypeStruct((tiles, 2 * tile), jnp.float32),
        ),
        in_specs=[
            pl.BlockSpec(memory_space=pl.ANY),
            pl.BlockSpec(memory_space=pltpu.VMEM),
            pl.BlockSpec(memory_space=pltpu.VMEM),
        ],
        out_specs=(pl.BlockSpec(memory_space=pl.ANY), pl.BlockSpec(memory_space=pltpu.VMEM)),
        scratch_shapes=[
            pltpu.SemaphoreType.DMA,
            pltpu.SemaphoreType.DMA((n_col,)),
            pltpu.SemaphoreType.DMA((max(planes - 1, 1), n_col)),
            pltpu.SemaphoreType.DMA((planes, n_col)),
            pltpu.SemaphoreType.DMA((n_row, n_col)),
        ],
        compiler_params=pltpu.CompilerParams(
            collective_id=1, has_side_effects=True, vmem_limit_bytes=32 * 1024 * 1024
        ),
    )(amp_owned, pairs, places)


def on_device(amp_owned, pair_of_slot, amp_tiles, integrals, integral_tile_mask):
    n_col = lax.axis_size("col")
    n_row = lax.axis_size("row")
    col_at = lax.axis_index("col")
    row_at = lax.axis_index("row")
    own_rows, width_all = amp_owned.shape
    total_rows = pair_of_slot.shape[0]
    grid_rows = total_rows // n_row
    sections, slab_rows, out_cols = integrals.shape
    tile_size = total_rows // amp_tiles.shape[0]
    piece_cols = width_all // n_col
    row_tiles = grid_rows // tile_size
    piece_tiles = piece_cols // tile_size

    local_tile_rows = slab_rows // tile_size
    col_tiles = out_cols // tile_size
    tiles_int = lax.dynamic_slice(
        integral_tile_mask,
        (0, row_at * local_tile_rows, col_at * col_tiles),
        (sections, local_tile_rows, col_tiles),
    )
    factors = jnp.repeat(
        tiles_int.reshape(sections * local_tile_rows, col_tiles).astype(jnp.bfloat16), tile_size, axis=1
    )

    slot = jnp.arange(total_rows, dtype=jnp.int32)
    owner, within = slot // own_rows, slot % own_rows
    place = ((owner % n_row) * n_col + owner // n_row) * own_rows + within
    places = jnp.stack([place // 128, place % 128]).astype(jnp.float32)
    everyone, found = deal(amp_owned, pair_of_slot[None, :], places, n_row, n_col, tile_size)
    everyone = everyone.reshape(total_rows, piece_cols)
    found = found.astype(jnp.int32)
    found = (found[:, :tile_size] * 128 + found[:, tile_size:]).reshape(grid_rows)

    my_tiles = lax.dynamic_slice(
        amp_tiles, (row_at * row_tiles, col_at * piece_tiles), (row_tiles, piece_tiles)
    )
    amp_piece = apply_tile_blocks(
        everyone.at[found].get(mode="promise_in_bounds"), my_tiles, tile_size
    )
    return spread_multiply(amp_piece, integrals, factors, n_col, n_row, tile_size)


def solution(mesh):
    placed = (P(("col", "row"), None), P(), P(), P(None, "row", "col"), P())
    return jax.shard_map(
        on_device, mesh=mesh, in_specs=placed, out_specs=P("row", "col"), check_vma=False
    )
```

```python
import functools

import jax
import jax.numpy as jnp
from jax import lax
from jax.experimental import pallas as pl
from jax.experimental.pallas import tpu as pltpu
from jax.sharding import PartitionSpec as P

MESH = pl.DeviceIdType.MESH


def apply_tile_blocks(block_data, tile_map, tile_size):
    row_count, col_count = block_data.shape
    shaped = block_data.reshape(
        row_count // tile_size, tile_size, col_count // tile_size, tile_size
    )
    shaped = shaped * tile_map.astype(block_data.dtype)[:, None, :, None]
    return shaped.reshape(row_count, col_count)


def spread_kernel(
    lines,
    width,
    n_row,
    chunk,
    tile,
    a_ref,
    i_ref,
    m_ref,
    o_ref,
    full,
    b_ref,
    load,
    zsend,
    zrecv,
    xsend,
    xrecv,
    bsend,
    bcore,
    brecv,
):
    col = lax.axis_index("col")
    row = lax.axis_index("row")
    planes = n_row // 2
    sections, slab_rows, _ = i_ref.shape
    core = row % 2
    partner = row + 1 - 2 * core
    z, x = col // width, col % width
    rows = a_ref.shape[0]
    chunks = rows // chunk
    paired = chunks // 6 if width == 2 else 0
    beats = chunks + paired
    out_cols = o_ref.shape[1]

    barrier = pltpu.get_barrier_semaphore()
    for side in (1, -1):
        near = z + side

        @pl.when((near >= 0) & (near < lines))
        def _(near=near):
            pl.semaphore_signal(
                barrier, inc=1, device_id={"col": near * width + x}, device_id_type=MESH
            )

    for e in range(1, width):
        pl.semaphore_signal(
            barrier, inc=1, device_id={"col": z * width + (x + e) % width}, device_id_type=MESH
        )
    pl.semaphore_signal(barrier, inc=1, device_id={"row": partner}, device_id_type=MESH)
    for e in range(1, planes):
        pl.semaphore_signal(
            barrier, inc=1, device_id={"row": (row + 2 * e) % n_row}, device_id_type=MESH
        )

    own = pltpu.make_async_copy(a_ref, full.at[col], load)
    own.start()
    tiles = slab_rows // tile
    for s in range(sections):
        for i in range(tiles):
            at = slice(i * tile, (i + 1) * tile)
            b_ref[s * n_row + row, at, :] = (
                i_ref[s, at, :] * m_ref[s * tiles + i : s * tiles + i + 1, :]
            )
    ends = (z == 0).astype(jnp.int32) + (z == lines - 1).astype(jnp.int32)
    pl.semaphore_wait(barrier, width + 1 - ends + planes)
    own.wait()

    def sent(s, held, to, sem):
        k = s * n_row + held
        return pltpu.make_async_remote_copy(
            src_ref=b_ref.at[k],
            dst_ref=b_ref.at[k],
            send_sem=sem,
            recv_sem=brecv.at[k],
            device_id={"row": to},
            device_id_type=MESH,
        )

    def beside(s, e):
        return sent(s, row, (row + 2 * e) % n_row, bsend.at[e - 1, s])

    def inside(s, e):
        held = (row + 2 * e) % n_row
        return sent(s, held, partner, bcore.at[e, s])

    def arrival(s, held):
        return sent(s, held, partner, bcore.at[0, s])

    def place(origin, v):
        k = origin * width + jnp.where(v < chunks, x, (x + 1) % width)
        return k, jnp.where(v < chunks, v, v - chunks)

    def along(origin, v, side):
        k, j = place(origin, v)
        piece = full.at[k, pl.ds(pl.multiple_of(j * chunk, chunk), chunk)]
        return pltpu.make_async_remote_copy(
            src_ref=piece,
            dst_ref=piece,
            send_sem=zsend.at[0 if side > 0 else 1, origin, v],
            recv_sem=zrecv.at[origin, v],
            device_id={"col": (z + side) * width + x},
            device_id_type=MESH,
        )

    def across(origin, j, e, which=None):
        held = x if which is None else which
        piece = full.at[origin * width + held, pl.ds(pl.multiple_of(j * chunk, chunk), chunk)]
        return pltpu.make_async_remote_copy(
            src_ref=piece,
            dst_ref=piece,
            send_sem=xsend.at[e - 1, origin, j],
            recv_sem=xrecv.at[origin * width + held, j],
            device_id={"col": z * width + (x + e) % width},
            device_id_type=MESH,
        )

    def multiply(k, j, first=False):
        at = pl.ds(pl.multiple_of(j * chunk, chunk), chunk)

        def part(n, carry):
            cols = pl.ds(pl.multiple_of(n * 512, 512), 512)
            term = 0.5 * jnp.dot(
                full[k, at, :], b_ref[k, :, cols], preferred_element_type=jnp.float32
            )
            if first:
                o_ref[at, cols] = term
            else:
                o_ref[at, cols] += term
            return carry

        lax.fori_loop(0, out_cols // 512, part, 0)

    def step(t, carry):
        d, j = t // beats, t % beats

        @pl.when(d == 0)
        def _():
            @pl.when(j < chunks)
            def _():
                for e in range(1, width):
                    across(z, j, e).start()

            if paired:

                @pl.when(j >= chunks)
                def _():
                    across(z, j - chunks, 1, (x + 1) % width).wait_recv()

            for side in (1, -1):

                @pl.when((z + side >= 0) & (z + side < lines))
                def _(side=side):
                    along(z, j, side).start()

        for s in range(sections):

            @pl.when(t == s)
            def _(s=s):
                for e in range(1, planes):
                    beside(s, e).start()
                inside(s, 0).start()

        for side in (1, -1):
            origin = z - side * d

            @pl.when((d > 0) & (d < lines) & (origin >= 0) & (origin < lines))
            def _(side=side, origin=origin):
                along(origin, j, -side).wait_recv()

                @pl.when((z + side >= 0) & (z + side < lines))
                def _():
                    along(origin, j, side).start()

                @pl.when((j >= paired) & (j < chunks))
                def _():
                    for e in range(1, width):
                        across(origin, j, e).start()

        for s in range(sections):

            @pl.when(t == beats + (s + 1) * beats // sections - 1)
            def _(s=s):
                for e in range(1, planes):
                    arrival(s, (row + 2 * e) % n_row).wait_recv()
                    inside(s, e).start()

        @pl.when(t == 2 * beats)
        def _():
            for s in range(sections):
                for e in range(planes):
                    arrival(s, (partner + 2 * e) % n_row).wait_recv()

        @pl.when((d == 2) & (j < chunks))
        def _():
            multiply(col, j, True)

        def lagged(apart):
            for side in (1, -1):
                origin = z - side * apart

                @pl.when((apart < lines) & (origin >= 0) & (origin < lines))
                def _(origin=origin):
                    multiply(*place(origin, j))

        def crossed(apart):
            for side in (1, -1):
                origin = z - side * apart
                due = True if side > 0 else apart > 0
                due = due & (j < chunks) & ((apart == 0) | (j >= paired))

                @pl.when(due & (origin >= 0) & (origin < lines))
                def _(origin=origin):
                    for e in range(1, width):
                        there = (x + e) % width

                        @pl.when(j >= paired)
                        def _(e=e, there=there):
                            across(origin, j, e, there).wait_recv()

                        multiply(origin * width + there, j)

        def late(i, carry):
            lagged(i)
            crossed(i - 1)
            return carry

        lax.fori_loop(jnp.where(d == 2, 1, d), jnp.where(d < 2, d, d + 1), late, 0)
        return carry

    lax.fori_loop(0, (lines + 1) * beats, step, 0)

    def drain(t, carry):
        origin, j = t // beats, t % beats

        @pl.when((origin <= z) & (z < lines - 1))
        def _():
            along(origin, j, 1).wait_send()

        @pl.when((origin >= z) & (z > 0))
        def _():
            along(origin, j, -1).wait_send()

        @pl.when((j < chunks) & ((origin == z) | (j >= paired)))
        def _():
            for e in range(1, width):
                across(origin, j, e).wait_send()

        return carry

    lax.fori_loop(0, lines * beats, drain, 0)
    for s in range(sections):
        for e in range(1, planes):
            beside(s, e).wait_send()
        for e in range(planes):
            inside(s, e).wait_send()


def spread_multiply(amp_piece, integrals, factors, n_col, n_row, tile):
    lines = 4 if n_col % 4 == 0 else n_col
    width = n_col // lines
    rows, depth = amp_piece.shape
    sections, slab_rows, out_cols = integrals.shape
    planes = n_row // 2
    chunk = 384 if rows % 384 == 0 else rows
    chunks = rows // chunk
    beats = chunks + (chunks // 6 if width == 2 else 0)
    return pl.pallas_call(
        functools.partial(spread_kernel, lines, width, n_row, chunk, tile),
        out_shape=jax.ShapeDtypeStruct((rows, out_cols), jnp.float32),
        in_specs=[
            pl.BlockSpec(memory_space=pl.ANY),
            pl.BlockSpec(memory_space=pltpu.VMEM),
            pl.BlockSpec(memory_space=pltpu.VMEM),
        ],
        out_specs=pl.BlockSpec(memory_space=pltpu.VMEM),
        scratch_shapes=[
            pltpu.VMEM((n_col, rows, depth), jnp.bfloat16),
            pltpu.VMEM((sections * n_row, slab_rows, out_cols), jnp.bfloat16),
            pltpu.SemaphoreType.DMA,
            pltpu.SemaphoreType.DMA((2, lines, beats)),
            pltpu.SemaphoreType.DMA((lines, beats)),
            pltpu.SemaphoreType.DMA((max(width - 1, 1), lines, chunks)),
            pltpu.SemaphoreType.DMA((n_col, chunks)),
            pltpu.SemaphoreType.DMA((max(planes - 1, 1), sections)),
            pltpu.SemaphoreType.DMA((planes, sections)),
            pltpu.SemaphoreType.DMA((sections * n_row,)),
        ],
        compiler_params=pltpu.CompilerParams(
            collective_id=0, has_side_effects=True, vmem_limit_bytes=58 * 1024 * 1024
        ),
        cost_estimate=pl.CostEstimate(
            flops=2 * rows * depth * n_col * out_cols, bytes_accessed=40_000_000, transcendentals=0
        ),
    )(amp_piece, integrals, factors)


def deal_kernel(
    n_row, n_col, tile, a_ref, pair_ref, place_ref, out_ref, found_ref, keep, asend, ysend, csend, recv
):
    col = lax.axis_index("col")
    row = lax.axis_index("row")
    planes = n_row // 2
    partner = row + 1 - 2 * (row % 2)
    _, _, own_rows, width = out_ref.shape

    barrier = pltpu.get_barrier_semaphore()
    for e in range(1, n_col):
        pl.semaphore_signal(
            barrier, inc=1, device_id={"col": (col + e) % n_col}, device_id_type=MESH
        )
    pl.semaphore_signal(barrier, inc=1, device_id={"row": partner}, device_id_type=MESH)
    for e in range(1, planes):
        pl.semaphore_signal(
            barrier, inc=1, device_id={"row": (row + 2 * e) % n_row}, device_id_type=MESH
        )
    pl.semaphore_wait(barrier, n_col + planes - 1)

    def cut(c):
        return a_ref.at[:, pl.ds(pl.multiple_of(c * width, width), width)]

    def dealt(e):
        to = (col + e) % n_col
        return pltpu.make_async_remote_copy(
            src_ref=cut(to),
            dst_ref=out_ref.at[row, col],
            send_sem=asend.at[e],
            recv_sem=recv.at[row, col],
            device_id={"col": to},
            device_id_type=MESH,
        )

    def sent(held, c, to, sem, src=None):
        return pltpu.make_async_remote_copy(
            src_ref=out_ref.at[held, c] if src is None else src,
            dst_ref=out_ref.at[held, c],
            send_sem=sem,
            recv_sem=recv.at[held, c],
            device_id={"row": to},
            device_id_type=MESH,
        )

    def beside(c, e, src=None):
        return sent(row, c, (row + 2 * e) % n_row, ysend.at[e - 1, c], src)

    def inside(c, e, src=None):
        return sent((row + 2 * e) % n_row, c, partner, csend.at[e, c], src)

    mine = pltpu.make_async_copy(cut(col), out_ref.at[row, col], keep)
    mine.start()
    for e in range(1, planes):
        beside(col, e, cut(col)).start()

    def start(e, carry):
        dealt(e).start()
        return carry

    lax.fori_loop(1, n_col, start, 0)
    inside(col, 0, cut(col)).start()

    total = pair_ref.shape[1]
    tiles = found_ref.shape[0]
    block = total // 8
    found_ref[...] = jnp.zeros_like(found_ref)

    def invert(i, carry):
        at = pl.ds(pl.multiple_of(i * block, block), block)
        pairs = pair_ref[:, at]
        here = lax.broadcasted_iota(jnp.int32, (tiles, block), 0) * tile + row * (tiles * tile)
        high = jnp.where((pairs >= here) & (pairs < here + tile), 1.0, 0.0).astype(jnp.bfloat16)
        low = (pairs & (tile - 1)) == lax.broadcasted_iota(jnp.int32, (tile, block), 0)
        for half in range(2):
            value = jnp.where(low, place_ref[half : half + 1, at], 0.0).astype(jnp.bfloat16)
            found_ref[:, half * tile : (half + 1) * tile] += lax.dot_general(
                high, value, (((1,), (1,)), ((), ())), preferred_element_type=jnp.float32
            )
        return carry

    lax.fori_loop(0, 8, invert, 0)

    def step(e, carry):
        @pl.when((e > 0) & (e < n_col))
        def _():
            c = (col + n_col - e) % n_col
            sent(row, c, partner, csend.at[0, c]).wait_recv()
            for f in range(1, planes):
                beside(c, f).start()
            inside(c, 0).start()

        @pl.when(e > 0)
        def _():
            c = (col + n_col - (e - 1)) % n_col
            for f in range(1, planes):
                sent((row + 2 * f) % n_row, c, partner, csend.at[f, c]).wait_recv()
                inside(c, f).start()

        return carry

    lax.fori_loop(0, n_col + 1, step, 0)
    mine.wait()

    def drain(c, carry):
        for f in range(planes):
            sent((partner + 2 * f) % n_row, c, partner, csend.at[f, c]).wait_recv()
            inside(c, f).wait_send()
        for f in range(1, planes):
            beside(c, f).wait_send()

        @pl.when(c > 0)
        def _():
            dealt(c).wait_send()

        return carry

    lax.fori_loop(0, n_col, drain, 0)


def deal(amp_owned, pairs, places, n_row, n_col, tile):
    own_rows, width_all = amp_owned.shape
    tiles = pairs.shape[1] // n_row // tile
    planes = n_row // 2
    return pl.pallas_call(
        functools.partial(deal_kernel, n_row, n_col, tile),
        out_shape=(
            jax.ShapeDtypeStruct((n_row, n_col, own_rows, width_all // n_col), jnp.bfloat16),
            jax.ShapeDtypeStruct((tiles, 2 * tile), jnp.float32),
        ),
        in_specs=[
            pl.BlockSpec(memory_space=pl.ANY),
            pl.BlockSpec(memory_space=pltpu.VMEM),
            pl.BlockSpec(memory_space=pltpu.VMEM),
        ],
        out_specs=(pl.BlockSpec(memory_space=pl.ANY), pl.BlockSpec(memory_space=pltpu.VMEM)),
        scratch_shapes=[
            pltpu.SemaphoreType.DMA,
            pltpu.SemaphoreType.DMA((n_col,)),
            pltpu.SemaphoreType.DMA((max(planes - 1, 1), n_col)),
            pltpu.SemaphoreType.DMA((planes, n_col)),
            pltpu.SemaphoreType.DMA((n_row, n_col)),
        ],
        compiler_params=pltpu.CompilerParams(
            collective_id=1, has_side_effects=True, vmem_limit_bytes=32 * 1024 * 1024
        ),
    )(amp_owned, pairs, places)


def on_device(amp_owned, pair_of_slot, amp_tiles, integrals, integral_tile_mask):
    n_col = lax.axis_size("col")
    n_row = lax.axis_size("row")
    col_at = lax.axis_index("col")
    row_at = lax.axis_index("row")
    own_rows, width_all = amp_owned.shape
    total_rows = pair_of_slot.shape[0]
    grid_rows = total_rows // n_row
    sections, slab_rows, out_cols = integrals.shape
    tile_size = total_rows // amp_tiles.shape[0]
    piece_cols = width_all // n_col
    row_tiles = grid_rows // tile_size
    piece_tiles = piece_cols // tile_size

    local_tile_rows = slab_rows // tile_size
    col_tiles = out_cols // tile_size
    tiles_int = lax.dynamic_slice(
        integral_tile_mask,
        (0, row_at * local_tile_rows, col_at * col_tiles),
        (sections, local_tile_rows, col_tiles),
    )
    factors = jnp.repeat(
        tiles_int.reshape(sections * local_tile_rows, col_tiles).astype(jnp.bfloat16), tile_size, axis=1
    )

    slot = jnp.arange(total_rows, dtype=jnp.int32)
    owner, within = slot // own_rows, slot % own_rows
    place = ((owner % n_row) * n_col + owner // n_row) * own_rows + within
    places = jnp.stack([place // 128, place % 128]).astype(jnp.float32)
    everyone, found = deal(amp_owned, pair_of_slot[None, :], places, n_row, n_col, tile_size)
    everyone = everyone.reshape(total_rows, piece_cols)
    found = found.astype(jnp.int32)
    found = (found[:, :tile_size] * 128 + found[:, tile_size:]).reshape(grid_rows)

    my_tiles = lax.dynamic_slice(
        amp_tiles, (row_at * row_tiles, col_at * piece_tiles), (row_tiles, piece_tiles)
    )
    amp_piece = apply_tile_blocks(
        everyone.at[found].get(mode="promise_in_bounds"), my_tiles, tile_size
    )
    return spread_multiply(amp_piece, integrals, factors, n_col, n_row, tile_size)


def solution(mesh):
    placed = (P(("col", "row"), None), P(), P(), P(None, "row", "col"), P())
    return jax.shard_map(
        on_device, mesh=mesh, in_specs=placed, out_specs=P("row", "col"), check_vma=False
    )
```

```python
import functools

import jax
import jax.numpy as jnp
from jax import lax
from jax.experimental import pallas as pl
from jax.experimental.pallas import tpu as pltpu
from jax.sharding import PartitionSpec as P

MESH = pl.DeviceIdType.MESH


def apply_tile_blocks(block_data, tile_map, tile_size):
    row_count, col_count = block_data.shape
    shaped = block_data.reshape(
        row_count // tile_size, tile_size, col_count // tile_size, tile_size
    )
    shaped = shaped * tile_map.astype(block_data.dtype)[:, None, :, None]
    return shaped.reshape(row_count, col_count)


def spread_kernel(
    lines,
    width,
    n_row,
    chunk,
    tile,
    a_ref,
    i_ref,
    m_ref,
    o_ref,
    full,
    b_ref,
    load,
    zsend,
    zrecv,
    xsend,
    xrecv,
    bsend,
    bcore,
    brecv,
):
    col = lax.axis_index("col")
    row = lax.axis_index("row")
    planes = n_row // 2
    sections, slab_rows, _ = i_ref.shape
    core = row % 2
    partner = row + 1 - 2 * core
    z, x = col // width, col % width
    rows = a_ref.shape[0]
    chunks = rows // chunk
    paired = chunks // 6 if width == 2 else 0
    beats = chunks + paired
    out_cols = o_ref.shape[1]

    barrier = pltpu.get_barrier_semaphore()
    for side in (1, -1):
        near = z + side

        @pl.when((near >= 0) & (near < lines))
        def _(near=near):
            pl.semaphore_signal(
                barrier, inc=1, device_id={"col": near * width + x}, device_id_type=MESH
            )

    for e in range(1, width):
        pl.semaphore_signal(
            barrier, inc=1, device_id={"col": z * width + (x + e) % width}, device_id_type=MESH
        )
    pl.semaphore_signal(barrier, inc=1, device_id={"row": partner}, device_id_type=MESH)
    for e in range(1, planes):
        pl.semaphore_signal(
            barrier, inc=1, device_id={"row": (row + 2 * e) % n_row}, device_id_type=MESH
        )

    own = pltpu.make_async_copy(a_ref, full.at[col], load)
    own.start()
    tiles = slab_rows // tile
    for s in range(sections):
        for i in range(tiles):
            at = slice(i * tile, (i + 1) * tile)
            b_ref[s * n_row + row, at, :] = (
                i_ref[s, at, :] * m_ref[s * tiles + i : s * tiles + i + 1, :]
            )
    ends = (z == 0).astype(jnp.int32) + (z == lines - 1).astype(jnp.int32)
    pl.semaphore_wait(barrier, width + 1 - ends + planes)
    own.wait()

    def sent(s, held, to, sem):
        k = s * n_row + held
        return pltpu.make_async_remote_copy(
            src_ref=b_ref.at[k],
            dst_ref=b_ref.at[k],
            send_sem=sem,
            recv_sem=brecv.at[k],
            device_id={"row": to},
            device_id_type=MESH,
        )

    def beside(s, e):
        return sent(s, row, (row + 2 * e) % n_row, bsend.at[e - 1, s])

    def inside(s, e):
        held = (row + 2 * e) % n_row
        return sent(s, held, partner, bcore.at[e, s])

    def arrival(s, held):
        return sent(s, held, partner, bcore.at[0, s])

    def place(origin, v):
        k = origin * width + jnp.where(v < chunks, x, (x + 1) % width)
        return k, jnp.where(v < chunks, v, v - chunks)

    def along(origin, v, side):
        k, j = place(origin, v)
        piece = full.at[k, pl.ds(pl.multiple_of(j * chunk, chunk), chunk)]
        return pltpu.make_async_remote_copy(
            src_ref=piece,
            dst_ref=piece,
            send_sem=zsend.at[0 if side > 0 else 1, origin, v],
            recv_sem=zrecv.at[origin, v],
            device_id={"col": (z + side) * width + x},
            device_id_type=MESH,
        )

    def across(origin, j, e, which=None):
        held = x if which is None else which
        piece = full.at[origin * width + held, pl.ds(pl.multiple_of(j * chunk, chunk), chunk)]
        return pltpu.make_async_remote_copy(
            src_ref=piece,
            dst_ref=piece,
            send_sem=xsend.at[e - 1, origin, j],
            recv_sem=xrecv.at[origin * width + held, j],
            device_id={"col": z * width + (x + e) % width},
            device_id_type=MESH,
        )

    def multiply(k, j, first=False):
        at = pl.ds(pl.multiple_of(j * chunk, chunk), chunk)

        def part(n, carry):
            cols = pl.ds(pl.multiple_of(n * 512, 512), 512)
            term = jnp.dot(
                full[k, at, :], b_ref[k, :, cols], preferred_element_type=jnp.float32
            )
            if first:
                o_ref[at, cols] = term
            else:
                o_ref[at, cols] += term
            return carry

        lax.fori_loop(0, out_cols // 512, part, 0)

    def step(t, carry):
        d, j = t // beats, t % beats

        @pl.when(d == 0)
        def _():
            @pl.when(j < chunks)
            def _():
                for e in range(1, width):
                    across(z, j, e).start()

            if paired:

                @pl.when(j >= chunks)
                def _():
                    across(z, j - chunks, 1, (x + 1) % width).wait_recv()

            for side in (1, -1):

                @pl.when((z + side >= 0) & (z + side < lines))
                def _(side=side):
                    along(z, j, side).start()

        for s in range(sections):

            @pl.when(t == s)
            def _(s=s):
                for e in range(1, planes):
                    beside(s, e).start()
                inside(s, 0).start()

        for side in (1, -1):
            origin = z - side * d

            @pl.when((d > 0) & (d < lines) & (origin >= 0) & (origin < lines))
            def _(side=side, origin=origin):
                along(origin, j, -side).wait_recv()

                @pl.when((z + side >= 0) & (z + side < lines))
                def _():
                    along(origin, j, side).start()

                @pl.when((j >= paired) & (j < chunks))
                def _():
                    for e in range(1, width):
                        across(origin, j, e).start()

        for s in range(sections):

            @pl.when(t == beats + (s + 1) * beats // sections - 1)
            def _(s=s):
                for e in range(1, planes):
                    arrival(s, (row + 2 * e) % n_row).wait_recv()
                    inside(s, e).start()

        @pl.when(t == 2 * beats)
        def _():
            for s in range(sections):
                for e in range(planes):
                    arrival(s, (partner + 2 * e) % n_row).wait_recv()

        @pl.when((d == 2) & (j < chunks))
        def _():
            multiply(col, j, True)

        def lagged(apart):
            for side in (1, -1):
                origin = z - side * apart

                @pl.when((apart < lines) & (origin >= 0) & (origin < lines))
                def _(origin=origin):
                    multiply(*place(origin, j))

        def crossed(apart):
            for side in (1, -1):
                origin = z - side * apart
                due = True if side > 0 else apart > 0
                due = due & (j < chunks) & ((apart == 0) | (j >= paired))

                @pl.when(due & (origin >= 0) & (origin < lines))
                def _(origin=origin):
                    for e in range(1, width):
                        there = (x + e) % width

                        @pl.when(j >= paired)
                        def _(e=e, there=there):
                            across(origin, j, e, there).wait_recv()

                        multiply(origin * width + there, j)

        def late(i, carry):
            lagged(i)
            crossed(i - 1)
            return carry

        lax.fori_loop(jnp.where(d == 2, 1, d), jnp.where(d < 2, d, d + 1), late, 0)
        return carry

    lax.fori_loop(0, (lines + 1) * beats, step, 0)

    def drain(t, carry):
        origin, j = t // beats, t % beats

        @pl.when((origin <= z) & (z < lines - 1))
        def _():
            along(origin, j, 1).wait_send()

        @pl.when((origin >= z) & (z > 0))
        def _():
            along(origin, j, -1).wait_send()

        @pl.when((j < chunks) & ((origin == z) | (j >= paired)))
        def _():
            for e in range(1, width):
                across(origin, j, e).wait_send()

        return carry

    lax.fori_loop(0, lines * beats, drain, 0)
    for s in range(sections):
        for e in range(1, planes):
            beside(s, e).wait_send()
        for e in range(planes):
            inside(s, e).wait_send()


def spread_multiply(amp_piece, integrals, factors, n_col, n_row, tile):
    lines = 4 if n_col % 4 == 0 else n_col
    width = n_col // lines
    rows, depth = amp_piece.shape
    sections, slab_rows, out_cols = integrals.shape
    planes = n_row // 2
    chunk = 384 if rows % 384 == 0 else rows
    chunks = rows // chunk
    beats = chunks + (chunks // 6 if width == 2 else 0)
    return pl.pallas_call(
        functools.partial(spread_kernel, lines, width, n_row, chunk, tile),
        out_shape=pltpu.VMEM((rows, out_cols), jnp.float32),
        in_specs=[
            pl.BlockSpec(memory_space=pl.ANY),
            pl.BlockSpec(memory_space=pltpu.VMEM),
            pl.BlockSpec(memory_space=pltpu.VMEM),
        ],
        out_specs=pl.BlockSpec(memory_space=pltpu.VMEM),
        scratch_shapes=[
            pltpu.VMEM((n_col, rows, depth), jnp.bfloat16),
            pltpu.VMEM((sections * n_row, slab_rows, out_cols), jnp.bfloat16),
            pltpu.SemaphoreType.DMA,
            pltpu.SemaphoreType.DMA((2, lines, beats)),
            pltpu.SemaphoreType.DMA((lines, beats)),
            pltpu.SemaphoreType.DMA((max(width - 1, 1), lines, chunks)),
            pltpu.SemaphoreType.DMA((n_col, chunks)),
            pltpu.SemaphoreType.DMA((max(planes - 1, 1), sections)),
            pltpu.SemaphoreType.DMA((planes, sections)),
            pltpu.SemaphoreType.DMA((sections * n_row,)),
        ],
        compiler_params=pltpu.CompilerParams(
            collective_id=0, has_side_effects=True, vmem_limit_bytes=44 * 1024 * 1024
        ),
        cost_estimate=pl.CostEstimate(
            flops=2 * rows * depth * n_col * out_cols, bytes_accessed=40_000_000, transcendentals=0
        ),
    )(amp_piece, integrals, factors)


def deal_kernel(
    n_row, n_col, tile, a_ref, pair_ref, place_ref, out_ref, found_ref, keep, asend, ysend, csend, recv
):
    col = lax.axis_index("col")
    row = lax.axis_index("row")
    planes = n_row // 2
    partner = row + 1 - 2 * (row % 2)
    _, _, own_rows, width = out_ref.shape

    barrier = pltpu.get_barrier_semaphore()
    for e in range(1, n_col):
        pl.semaphore_signal(
            barrier, inc=1, device_id={"col": (col + e) % n_col}, device_id_type=MESH
        )
    pl.semaphore_signal(barrier, inc=1, device_id={"row": partner}, device_id_type=MESH)
    for e in range(1, planes):
        pl.semaphore_signal(
            barrier, inc=1, device_id={"row": (row + 2 * e) % n_row}, device_id_type=MESH
        )
    pl.semaphore_wait(barrier, n_col + planes - 1)

    def cut(c):
        return a_ref.at[:, pl.ds(pl.multiple_of(c * width, width), width)]

    def dealt(e):
        to = (col + e) % n_col
        return pltpu.make_async_remote_copy(
            src_ref=cut(to),
            dst_ref=out_ref.at[row, col],
            send_sem=asend.at[e],
            recv_sem=recv.at[row, col],
            device_id={"col": to},
            device_id_type=MESH,
        )

    def sent(held, c, to, sem, src=None):
        return pltpu.make_async_remote_copy(
            src_ref=out_ref.at[held, c] if src is None else src,
            dst_ref=out_ref.at[held, c],
            send_sem=sem,
            recv_sem=recv.at[held, c],
            device_id={"row": to},
            device_id_type=MESH,
        )

    def beside(c, e, src=None):
        return sent(row, c, (row + 2 * e) % n_row, ysend.at[e - 1, c], src)

    def inside(c, e, src=None):
        return sent((row + 2 * e) % n_row, c, partner, csend.at[e, c], src)

    mine = pltpu.make_async_copy(cut(col), out_ref.at[row, col], keep)
    mine.start()
    for e in range(1, planes):
        beside(col, e, cut(col)).start()

    def start(e, carry):
        dealt(e).start()
        return carry

    lax.fori_loop(1, n_col, start, 0)
    inside(col, 0, cut(col)).start()

    total = pair_ref.shape[1]
    tiles = found_ref.shape[0]
    block = total // 8
    found_ref[...] = jnp.zeros_like(found_ref)

    def invert(i, carry):
        at = pl.ds(pl.multiple_of(i * block, block), block)
        pairs = pair_ref[:, at]
        here = lax.broadcasted_iota(jnp.int32, (tiles, block), 0) * tile + row * (tiles * tile)
        high = jnp.where((pairs >= here) & (pairs < here + tile), 1.0, 0.0).astype(jnp.bfloat16)
        low = (pairs & (tile - 1)) == lax.broadcasted_iota(jnp.int32, (tile, block), 0)
        for half in range(2):
            value = jnp.where(low, place_ref[half : half + 1, at], 0.0).astype(jnp.bfloat16)
            found_ref[:, half * tile : (half + 1) * tile] += lax.dot_general(
                high, value, (((1,), (1,)), ((), ())), preferred_element_type=jnp.float32
            )
        return carry

    lax.fori_loop(0, 8, invert, 0)

    def step(e, carry):
        @pl.when((e > 0) & (e < n_col))
        def _():
            c = (col + n_col - e) % n_col
            sent(row, c, partner, csend.at[0, c]).wait_recv()
            for f in range(1, planes):
                beside(c, f).start()
            inside(c, 0).start()

        @pl.when(e > 0)
        def _():
            c = (col + n_col - (e - 1)) % n_col
            for f in range(1, planes):
                sent((row + 2 * f) % n_row, c, partner, csend.at[f, c]).wait_recv()
                inside(c, f).start()

        return carry

    lax.fori_loop(0, n_col + 1, step, 0)
    mine.wait()

    def drain(c, carry):
        for f in range(planes):
            sent((partner + 2 * f) % n_row, c, partner, csend.at[f, c]).wait_recv()
            inside(c, f).wait_send()
        for f in range(1, planes):
            beside(c, f).wait_send()

        @pl.when(c > 0)
        def _():
            dealt(c).wait_send()

        return carry

    lax.fori_loop(0, n_col, drain, 0)


def deal(amp_owned, pairs, places, n_row, n_col, tile):
    own_rows, width_all = amp_owned.shape
    tiles = pairs.shape[1] // n_row // tile
    planes = n_row // 2
    return pl.pallas_call(
        functools.partial(deal_kernel, n_row, n_col, tile),
        out_shape=(
            jax.ShapeDtypeStruct((n_row, n_col, own_rows, width_all // n_col), jnp.bfloat16),
            jax.ShapeDtypeStruct((tiles, 2 * tile), jnp.float32),
        ),
        in_specs=[
            pl.BlockSpec(memory_space=pl.ANY),
            pl.BlockSpec(memory_space=pltpu.VMEM),
            pl.BlockSpec(memory_space=pltpu.VMEM),
        ],
        out_specs=(pl.BlockSpec(memory_space=pl.ANY), pl.BlockSpec(memory_space=pltpu.VMEM)),
        scratch_shapes=[
            pltpu.SemaphoreType.DMA,
            pltpu.SemaphoreType.DMA((n_col,)),
            pltpu.SemaphoreType.DMA((max(planes - 1, 1), n_col)),
            pltpu.SemaphoreType.DMA((planes, n_col)),
            pltpu.SemaphoreType.DMA((n_row, n_col)),
        ],
        compiler_params=pltpu.CompilerParams(
            collective_id=1, has_side_effects=True, vmem_limit_bytes=32 * 1024 * 1024
        ),
    )(amp_owned, pairs, places)


def on_device(amp_owned, pair_of_slot, amp_tiles, integrals, integral_tile_mask):
    n_col = lax.axis_size("col")
    n_row = lax.axis_size("row")
    col_at = lax.axis_index("col")
    row_at = lax.axis_index("row")
    own_rows, width_all = amp_owned.shape
    total_rows = pair_of_slot.shape[0]
    grid_rows = total_rows // n_row
    sections, slab_rows, out_cols = integrals.shape
    tile_size = total_rows // amp_tiles.shape[0]
    piece_cols = width_all // n_col
    row_tiles = grid_rows // tile_size
    piece_tiles = piece_cols // tile_size

    local_tile_rows = slab_rows // tile_size
    col_tiles = out_cols // tile_size
    tiles_int = lax.dynamic_slice(
        integral_tile_mask,
        (0, row_at * local_tile_rows, col_at * col_tiles),
        (sections, local_tile_rows, col_tiles),
    )
    factors = jnp.repeat(
        tiles_int.reshape(sections * local_tile_rows, col_tiles).astype(jnp.bfloat16), tile_size, axis=1
    )

    slot = jnp.arange(total_rows, dtype=jnp.int32)
    owner, within = slot // own_rows, slot % own_rows
    place = ((owner % n_row) * n_col + owner // n_row) * own_rows + within
    places = jnp.stack([place // 128, place % 128]).astype(jnp.float32)
    everyone, found = deal(amp_owned, pair_of_slot[None, :], places, n_row, n_col, tile_size)
    everyone = everyone.reshape(total_rows, piece_cols)
    found = found.astype(jnp.int32)
    found = (found[:, :tile_size] * 128 + found[:, tile_size:]).reshape(grid_rows)

    my_tiles = lax.dynamic_slice(
        amp_tiles, (row_at * row_tiles, col_at * piece_tiles), (row_tiles, piece_tiles)
    )
    amp_piece = apply_tile_blocks(
        everyone.at[found].get(mode="promise_in_bounds"), my_tiles, tile_size
    )
    return 0.5 * spread_multiply(amp_piece, integrals, factors, n_col, n_row, tile_size)


def solution(mesh):
    placed = (P(("col", "row"), None), P(), P(), P(None, "row", "col"), P())
    return jax.shard_map(
        on_device, mesh=mesh, in_specs=placed, out_specs=P("row", "col"), check_vma=False
    )
```

```python
import functools

import jax
import jax.numpy as jnp
from jax import lax
from jax.experimental import pallas as pl
from jax.experimental.pallas import tpu as pltpu
from jax.sharding import PartitionSpec as P

MESH = pl.DeviceIdType.MESH


def apply_tile_blocks(block_data, tile_map, tile_size):
    row_count, col_count = block_data.shape
    shaped = block_data.reshape(
        row_count // tile_size, tile_size, col_count // tile_size, tile_size
    )
    shaped = shaped * tile_map.astype(block_data.dtype)[:, None, :, None]
    return shaped.reshape(row_count, col_count)


def spread_kernel(
    lines,
    width,
    n_row,
    chunk,
    tile,
    a_ref,
    i_ref,
    m_ref,
    o_ref,
    full,
    b_ref,
    load,
    zsend,
    zrecv,
    xsend,
    xrecv,
    bsend,
    bcore,
    brecv,
):
    col = lax.axis_index("col")
    row = lax.axis_index("row")
    planes = n_row // 2
    sections, slab_rows, _ = i_ref.shape
    core = row % 2
    partner = row + 1 - 2 * core
    z, x = col // width, col % width
    rows = a_ref.shape[0]
    chunks = rows // chunk
    paired = chunks // 6 if width == 2 else 0
    beats = chunks + paired
    out_cols = o_ref.shape[1]

    barrier = pltpu.get_barrier_semaphore()
    for side in (1, -1):
        near = z + side

        @pl.when((near >= 0) & (near < lines))
        def _(near=near):
            pl.semaphore_signal(
                barrier, inc=1, device_id={"col": near * width + x}, device_id_type=MESH
            )

    for e in range(1, width):
        pl.semaphore_signal(
            barrier, inc=1, device_id={"col": z * width + (x + e) % width}, device_id_type=MESH
        )
    pl.semaphore_signal(barrier, inc=1, device_id={"row": partner}, device_id_type=MESH)
    for e in range(1, planes):
        pl.semaphore_signal(
            barrier, inc=1, device_id={"row": (row + 2 * e) % n_row}, device_id_type=MESH
        )

    own = pltpu.make_async_copy(a_ref, full.at[col], load)
    own.start()
    tiles = slab_rows // tile
    for s in range(sections):
        for i in range(tiles):
            at = slice(i * tile, (i + 1) * tile)
            b_ref[s * n_row + row, at, :] = (
                i_ref[s, at, :] * m_ref[s * tiles + i : s * tiles + i + 1, :]
            )
    ends = (z == 0).astype(jnp.int32) + (z == lines - 1).astype(jnp.int32)
    pl.semaphore_wait(barrier, width + 1 - ends + planes)
    own.wait()

    def sent(s, held, to, sem):
        k = s * n_row + held
        return pltpu.make_async_remote_copy(
            src_ref=b_ref.at[k],
            dst_ref=b_ref.at[k],
            send_sem=sem,
            recv_sem=brecv.at[k],
            device_id={"row": to},
            device_id_type=MESH,
        )

    def beside(s, e):
        return sent(s, row, (row + 2 * e) % n_row, bsend.at[e - 1, s])

    def inside(s, e):
        held = (row + 2 * e) % n_row
        return sent(s, held, partner, bcore.at[e, s])

    def arrival(s, held):
        return sent(s, held, partner, bcore.at[0, s])

    def place(origin, v):
        k = origin * width + jnp.where(v < chunks, x, (x + 1) % width)
        return k, jnp.where(v < chunks, v, v - chunks)

    def along(origin, v, side):
        k, j = place(origin, v)
        piece = full.at[k, pl.ds(pl.multiple_of(j * chunk, chunk), chunk)]
        return pltpu.make_async_remote_copy(
            src_ref=piece,
            dst_ref=piece,
            send_sem=zsend.at[0 if side > 0 else 1, origin, v],
            recv_sem=zrecv.at[origin, v],
            device_id={"col": (z + side) * width + x},
            device_id_type=MESH,
        )

    def across(origin, j, e, which=None):
        held = x if which is None else which
        piece = full.at[origin * width + held, pl.ds(pl.multiple_of(j * chunk, chunk), chunk)]
        return pltpu.make_async_remote_copy(
            src_ref=piece,
            dst_ref=piece,
            send_sem=xsend.at[e - 1, origin, j],
            recv_sem=xrecv.at[origin * width + held, j],
            device_id={"col": z * width + (x + e) % width},
            device_id_type=MESH,
        )

    def multiply(k, j, first=False):
        at = pl.ds(pl.multiple_of(j * chunk, chunk), chunk)

        def part(n, carry):
            cols = pl.ds(pl.multiple_of(n * 512, 512), 512)
            term = jnp.dot(
                full[k, at, :], b_ref[k, :, cols], preferred_element_type=jnp.float32
            )
            if first:
                o_ref[at, cols] = term
            else:
                o_ref[at, cols] += term
            return carry

        lax.fori_loop(0, out_cols // 512, part, 0)

    def step(t, carry):
        d, j = t // beats, t % beats

        @pl.when(d == 0)
        def _():
            @pl.when(j < chunks)
            def _():
                for e in range(1, width):
                    across(z, j, e).start()

            if paired:

                @pl.when(j >= chunks)
                def _():
                    across(z, j - chunks, 1, (x + 1) % width).wait_recv()

            for side in (1, -1):

                @pl.when((z + side >= 0) & (z + side < lines))
                def _(side=side):
                    along(z, j, side).start()

        for s in range(sections):

            @pl.when(t == s)
            def _(s=s):
                for e in range(1, planes):
                    beside(s, e).start()
                inside(s, 0).start()

        for side in (1, -1):
            origin = z - side * d

            @pl.when((d > 0) & (d < lines) & (origin >= 0) & (origin < lines))
            def _(side=side, origin=origin):
                along(origin, j, -side).wait_recv()

                @pl.when((z + side >= 0) & (z + side < lines))
                def _():
                    along(origin, j, side).start()

                @pl.when((j >= paired) & (j < chunks))
                def _():
                    for e in range(1, width):
                        across(origin, j, e).start()

        for s in range(sections):

            @pl.when(t == beats + (s + 1) * beats // sections - 1)
            def _(s=s):
                for e in range(1, planes):
                    arrival(s, (row + 2 * e) % n_row).wait_recv()
                    inside(s, e).start()

        @pl.when(t == 2 * beats)
        def _():
            for s in range(sections):
                for e in range(planes):
                    arrival(s, (partner + 2 * e) % n_row).wait_recv()

        @pl.when((d == 2) & (j < chunks))
        def _():
            multiply(col, j, True)

        def lagged(apart):
            for side in (1, -1):
                origin = z - side * apart

                @pl.when((apart < lines) & (origin >= 0) & (origin < lines))
                def _(origin=origin):
                    multiply(*place(origin, j))

        def crossed(apart):
            for side in (1, -1):
                origin = z - side * apart
                due = True if side > 0 else apart > 0
                due = due & (j < chunks) & ((apart == 0) | (j >= paired))

                @pl.when(due & (origin >= 0) & (origin < lines))
                def _(origin=origin):
                    for e in range(1, width):
                        there = (x + e) % width

                        @pl.when(j >= paired)
                        def _(e=e, there=there):
                            across(origin, j, e, there).wait_recv()

                        multiply(origin * width + there, j)

        def late(i, carry):
            lagged(i)
            crossed(i - 1)
            return carry

        lax.fori_loop(jnp.where(d == 2, 1, d), jnp.where(d < 2, d, d + 1), late, 0)
        return carry

    lax.fori_loop(0, (lines + 1) * beats, step, 0)

    def drain(t, carry):
        origin, j = t // beats, t % beats

        @pl.when((origin <= z) & (z < lines - 1))
        def _():
            along(origin, j, 1).wait_send()

        @pl.when((origin >= z) & (z > 0))
        def _():
            along(origin, j, -1).wait_send()

        @pl.when((j < chunks) & ((origin == z) | (j >= paired)))
        def _():
            for e in range(1, width):
                across(origin, j, e).wait_send()

        return carry

    lax.fori_loop(0, lines * beats, drain, 0)
    for s in range(sections):
        for e in range(1, planes):
            beside(s, e).wait_send()
        for e in range(planes):
            inside(s, e).wait_send()


def spread_multiply(amp_piece, integrals, factors, n_col, n_row, tile):
    lines = 4 if n_col % 4 == 0 else n_col
    width = n_col // lines
    rows, depth = amp_piece.shape
    sections, slab_rows, out_cols = integrals.shape
    planes = n_row // 2
    chunk = 192 if rows % 192 == 0 else rows
    chunks = rows // chunk
    beats = chunks + (chunks // 6 if width == 2 else 0)
    return pl.pallas_call(
        functools.partial(spread_kernel, lines, width, n_row, chunk, tile),
        out_shape=pltpu.VMEM((rows, out_cols), jnp.float32),
        in_specs=[
            pl.BlockSpec(memory_space=pl.ANY),
            pl.BlockSpec(memory_space=pltpu.VMEM),
            pl.BlockSpec(memory_space=pltpu.VMEM),
        ],
        out_specs=pl.BlockSpec(memory_space=pltpu.VMEM),
        scratch_shapes=[
            pltpu.VMEM((n_col, rows, depth), jnp.bfloat16),
            pltpu.VMEM((sections * n_row, slab_rows, out_cols), jnp.bfloat16),
            pltpu.SemaphoreType.DMA,
            pltpu.SemaphoreType.DMA((2, lines, beats)),
            pltpu.SemaphoreType.DMA((lines, beats)),
            pltpu.SemaphoreType.DMA((max(width - 1, 1), lines, chunks)),
            pltpu.SemaphoreType.DMA((n_col, chunks)),
            pltpu.SemaphoreType.DMA((max(planes - 1, 1), sections)),
            pltpu.SemaphoreType.DMA((planes, sections)),
            pltpu.SemaphoreType.DMA((sections * n_row,)),
        ],
        compiler_params=pltpu.CompilerParams(
            collective_id=0, has_side_effects=True, vmem_limit_bytes=44 * 1024 * 1024
        ),
        cost_estimate=pl.CostEstimate(
            flops=2 * rows * depth * n_col * out_cols, bytes_accessed=40_000_000, transcendentals=0
        ),
    )(amp_piece, integrals, factors)


def deal_kernel(
    n_row, n_col, tile, a_ref, pair_ref, place_ref, out_ref, found_ref, keep, asend, ysend, csend, recv
):
    col = lax.axis_index("col")
    row = lax.axis_index("row")
    planes = n_row // 2
    partner = row + 1 - 2 * (row % 2)
    _, _, own_rows, width = out_ref.shape

    barrier = pltpu.get_barrier_semaphore()
    for e in range(1, n_col):
        pl.semaphore_signal(
            barrier, inc=1, device_id={"col": (col + e) % n_col}, device_id_type=MESH
        )
    pl.semaphore_signal(barrier, inc=1, device_id={"row": partner}, device_id_type=MESH)
    for e in range(1, planes):
        pl.semaphore_signal(
            barrier, inc=1, device_id={"row": (row + 2 * e) % n_row}, device_id_type=MESH
        )
    pl.semaphore_wait(barrier, n_col + planes - 1)

    def cut(c):
        return a_ref.at[:, pl.ds(pl.multiple_of(c * width, width), width)]

    def dealt(e):
        to = (col + e) % n_col
        return pltpu.make_async_remote_copy(
            src_ref=cut(to),
            dst_ref=out_ref.at[row, col],
            send_sem=asend.at[e],
            recv_sem=recv.at[row, col],
            device_id={"col": to},
            device_id_type=MESH,
        )

    def sent(held, c, to, sem, src=None):
        return pltpu.make_async_remote_copy(
            src_ref=out_ref.at[held, c] if src is None else src,
            dst_ref=out_ref.at[held, c],
            send_sem=sem,
            recv_sem=recv.at[held, c],
            device_id={"row": to},
            device_id_type=MESH,
        )

    def beside(c, e, src=None):
        return sent(row, c, (row + 2 * e) % n_row, ysend.at[e - 1, c], src)

    def inside(c, e, src=None):
        return sent((row + 2 * e) % n_row, c, partner, csend.at[e, c], src)

    mine = pltpu.make_async_copy(cut(col), out_ref.at[row, col], keep)
    mine.start()
    for e in range(1, planes):
        beside(col, e, cut(col)).start()

    def start(e, carry):
        dealt(e).start()
        return carry

    lax.fori_loop(1, n_col, start, 0)
    inside(col, 0, cut(col)).start()

    total = pair_ref.shape[1]
    tiles = found_ref.shape[0]
    block = total // 8
    found_ref[...] = jnp.zeros_like(found_ref)

    def invert(i, carry):
        at = pl.ds(pl.multiple_of(i * block, block), block)
        pairs = pair_ref[:, at]
        here = lax.broadcasted_iota(jnp.int32, (tiles, block), 0) * tile + row * (tiles * tile)
        high = jnp.where((pairs >= here) & (pairs < here + tile), 1.0, 0.0).astype(jnp.bfloat16)
        low = (pairs & (tile - 1)) == lax.broadcasted_iota(jnp.int32, (tile, block), 0)
        for half in range(2):
            value = jnp.where(low, place_ref[half : half + 1, at], 0.0).astype(jnp.bfloat16)
            found_ref[:, half * tile : (half + 1) * tile] += lax.dot_general(
                high, value, (((1,), (1,)), ((), ())), preferred_element_type=jnp.float32
            )
        return carry

    lax.fori_loop(0, 8, invert, 0)

    def step(e, carry):
        @pl.when((e > 0) & (e < n_col))
        def _():
            c = (col + n_col - e) % n_col
            sent(row, c, partner, csend.at[0, c]).wait_recv()
            for f in range(1, planes):
                beside(c, f).start()
            inside(c, 0).start()

        @pl.when(e > 0)
        def _():
            c = (col + n_col - (e - 1)) % n_col
            for f in range(1, planes):
                sent((row + 2 * f) % n_row, c, partner, csend.at[f, c]).wait_recv()
                inside(c, f).start()

        return carry

    lax.fori_loop(0, n_col + 1, step, 0)
    mine.wait()

    def drain(c, carry):
        for f in range(planes):
            sent((partner + 2 * f) % n_row, c, partner, csend.at[f, c]).wait_recv()
            inside(c, f).wait_send()
        for f in range(1, planes):
            beside(c, f).wait_send()

        @pl.when(c > 0)
        def _():
            dealt(c).wait_send()

        return carry

    lax.fori_loop(0, n_col, drain, 0)


def deal(amp_owned, pairs, places, n_row, n_col, tile):
    own_rows, width_all = amp_owned.shape
    tiles = pairs.shape[1] // n_row // tile
    planes = n_row // 2
    return pl.pallas_call(
        functools.partial(deal_kernel, n_row, n_col, tile),
        out_shape=(
            pltpu.HBM((n_row, n_col, own_rows, width_all // n_col), jnp.bfloat16),
            jax.ShapeDtypeStruct((tiles, 2 * tile), jnp.float32),
        ),
        in_specs=[
            pl.BlockSpec(memory_space=pltpu.HBM),
            pl.BlockSpec(memory_space=pltpu.VMEM),
            pl.BlockSpec(memory_space=pltpu.VMEM),
        ],
        out_specs=(pl.BlockSpec(memory_space=pltpu.HBM), pl.BlockSpec(memory_space=pltpu.VMEM)),
        scratch_shapes=[
            pltpu.SemaphoreType.DMA,
            pltpu.SemaphoreType.DMA((n_col,)),
            pltpu.SemaphoreType.DMA((max(planes - 1, 1), n_col)),
            pltpu.SemaphoreType.DMA((planes, n_col)),
            pltpu.SemaphoreType.DMA((n_row, n_col)),
        ],
        compiler_params=pltpu.CompilerParams(
            collective_id=1, has_side_effects=True, vmem_limit_bytes=32 * 1024 * 1024
        ),
    )(amp_owned, pairs, places)


def on_device(amp_owned, pair_of_slot, amp_tiles, integrals, integral_tile_mask):
    n_col = lax.axis_size("col")
    n_row = lax.axis_size("row")
    col_at = lax.axis_index("col")
    row_at = lax.axis_index("row")
    own_rows, width_all = amp_owned.shape
    total_rows = pair_of_slot.shape[0]
    grid_rows = total_rows // n_row
    sections, slab_rows, out_cols = integrals.shape
    tile_size = total_rows // amp_tiles.shape[0]
    piece_cols = width_all // n_col
    row_tiles = grid_rows // tile_size
    piece_tiles = piece_cols // tile_size

    local_tile_rows = slab_rows // tile_size
    col_tiles = out_cols // tile_size
    tiles_int = lax.dynamic_slice(
        integral_tile_mask,
        (0, row_at * local_tile_rows, col_at * col_tiles),
        (sections, local_tile_rows, col_tiles),
    )
    factors = jnp.repeat(
        tiles_int.reshape(sections * local_tile_rows, col_tiles).astype(jnp.bfloat16), tile_size, axis=1
    )

    slot = jnp.arange(total_rows, dtype=jnp.int32)
    owner, within = slot // own_rows, slot % own_rows
    place = ((owner % n_row) * n_col + owner // n_row) * own_rows + within
    places = jnp.stack([place // 128, place % 128]).astype(jnp.float32)
    everyone, found = deal(amp_owned, pair_of_slot[None, :], places, n_row, n_col, tile_size)
    everyone = everyone.reshape(total_rows, piece_cols)
    found = found.astype(jnp.int32)
    found = (found[:, :tile_size] * 128 + found[:, tile_size:]).reshape(grid_rows)

    my_tiles = lax.dynamic_slice(
        amp_tiles, (row_at * row_tiles, col_at * piece_tiles), (row_tiles, piece_tiles)
    )
    amp_piece = apply_tile_blocks(
        everyone.at[found].get(mode="promise_in_bounds"), my_tiles, tile_size
    )
    return 0.5 * spread_multiply(amp_piece, integrals, factors, n_col, n_row, tile_size)


def solution(mesh):
    placed = (P(("col", "row"), None), P(), P(), P(None, "row", "col"), P())
    return jax.shard_map(
        on_device, mesh=mesh, in_specs=placed, out_specs=P("row", "col"), check_vma=False
    )
```

```python
import functools

import jax
import jax.numpy as jnp
from jax import lax
from jax.experimental import pallas as pl
from jax.experimental.pallas import tpu as pltpu
from jax.sharding import PartitionSpec as P

MESH = pl.DeviceIdType.MESH


def apply_tile_blocks(block_data, tile_map, tile_size):
    row_count, col_count = block_data.shape
    shaped = block_data.reshape(
        row_count // tile_size, tile_size, col_count // tile_size, tile_size
    )
    shaped = shaped * tile_map.astype(block_data.dtype)[:, None, :, None]
    return shaped.reshape(row_count, col_count)


def spread_kernel(
    lines,
    width,
    n_row,
    chunk,
    tile,
    a_ref,
    i_ref,
    m_ref,
    o_ref,
    full,
    b_ref,
    load,
    zsend,
    zrecv,
    xsend,
    xrecv,
    bsend,
    bcore,
    brecv,
):
    col = lax.axis_index("col")
    row = lax.axis_index("row")
    planes = n_row // 2
    sections, slab_rows, _ = i_ref.shape
    core = row % 2
    partner = row + 1 - 2 * core
    z, x = col // width, col % width
    rows = a_ref.shape[0]
    chunks = rows // chunk
    paired = chunks // 6 if width == 2 else 0
    beats = chunks + paired
    out_cols = o_ref.shape[1]

    barrier = pltpu.get_barrier_semaphore()
    for side in (1, -1):
        near = z + side

        @pl.when((near >= 0) & (near < lines))
        def _(near=near):
            pl.semaphore_signal(
                barrier, inc=1, device_id={"col": near * width + x}, device_id_type=MESH
            )

    for e in range(1, width):
        pl.semaphore_signal(
            barrier, inc=1, device_id={"col": z * width + (x + e) % width}, device_id_type=MESH
        )
    pl.semaphore_signal(barrier, inc=1, device_id={"row": partner}, device_id_type=MESH)
    for e in range(1, planes):
        pl.semaphore_signal(
            barrier, inc=1, device_id={"row": (row + 2 * e) % n_row}, device_id_type=MESH
        )

    own = pltpu.make_async_copy(a_ref, full.at[col], load)
    own.start()
    tiles = slab_rows // tile
    ends = (z == 0).astype(jnp.int32) + (z == lines - 1).astype(jnp.int32)
    pl.semaphore_wait(barrier, width + 1 - ends + planes)
    own.wait()

    def sent(s, held, to, sem):
        k = s * n_row + held
        return pltpu.make_async_remote_copy(
            src_ref=b_ref.at[k],
            dst_ref=b_ref.at[k],
            send_sem=sem,
            recv_sem=brecv.at[k],
            device_id={"row": to},
            device_id_type=MESH,
        )

    def beside(s, e):
        return sent(s, row, (row + 2 * e) % n_row, bsend.at[e - 1, s])

    def inside(s, e):
        held = (row + 2 * e) % n_row
        return sent(s, held, partner, bcore.at[e, s])

    def arrival(s, held):
        return sent(s, held, partner, bcore.at[0, s])

    def place(origin, v):
        k = origin * width + jnp.where(v < chunks, x, (x + 1) % width)
        return k, jnp.where(v < chunks, v, v - chunks)

    def along(origin, v, side):
        k, j = place(origin, v)
        piece = full.at[k, pl.ds(pl.multiple_of(j * chunk, chunk), chunk)]
        return pltpu.make_async_remote_copy(
            src_ref=piece,
            dst_ref=piece,
            send_sem=zsend.at[0 if side > 0 else 1, origin, v],
            recv_sem=zrecv.at[origin, v],
            device_id={"col": (z + side) * width + x},
            device_id_type=MESH,
        )

    def across(origin, j, e, which=None):
        held = x if which is None else which
        piece = full.at[origin * width + held, pl.ds(pl.multiple_of(j * chunk, chunk), chunk)]
        return pltpu.make_async_remote_copy(
            src_ref=piece,
            dst_ref=piece,
            send_sem=xsend.at[e - 1, origin, j],
            recv_sem=xrecv.at[origin * width + held, j],
            device_id={"col": z * width + (x + e) % width},
            device_id_type=MESH,
        )

    def multiply(k, j, first=False):
        at = pl.ds(pl.multiple_of(j * chunk, chunk), chunk)

        def part(n, carry):
            cols = pl.ds(pl.multiple_of(n * 512, 512), 512)
            term = jnp.dot(
                full[k, at, :], b_ref[k, :, cols], preferred_element_type=jnp.float32
            )
            if first:
                o_ref[at, cols] = term
            else:
                o_ref[at, cols] += term
            return carry

        lax.fori_loop(0, out_cols // 512, part, 0)

    def step(t, carry):
        d, j = t // beats, t % beats

        @pl.when(d == 0)
        def _():
            @pl.when(j < chunks)
            def _():
                for e in range(1, width):
                    across(z, j, e).start()

            if paired:

                @pl.when(j >= chunks)
                def _():
                    across(z, j - chunks, 1, (x + 1) % width).wait_recv()

            for side in (1, -1):

                @pl.when((z + side >= 0) & (z + side < lines))
                def _(side=side):
                    along(z, j, side).start()

        for s in range(sections):

            @pl.when(t == s)
            def _(s=s):
                for i in range(tiles):
                    at = slice(i * tile, (i + 1) * tile)
                    b_ref[s * n_row + row, at, :] = (
                        i_ref[s, at, :] * m_ref[s * tiles + i : s * tiles + i + 1, :]
                    )
                for e in range(1, planes):
                    beside(s, e).start()
                inside(s, 0).start()

        for side in (1, -1):
            origin = z - side * d

            @pl.when((d > 0) & (d < lines) & (origin >= 0) & (origin < lines))
            def _(side=side, origin=origin):
                along(origin, j, -side).wait_recv()

                @pl.when((z + side >= 0) & (z + side < lines))
                def _():
                    along(origin, j, side).start()

                @pl.when((j >= paired) & (j < chunks))
                def _():
                    for e in range(1, width):
                        across(origin, j, e).start()

        for s in range(sections):

            @pl.when(t == beats + (s + 1) * beats // sections - 1)
            def _(s=s):
                for e in range(1, planes):
                    arrival(s, (row + 2 * e) % n_row).wait_recv()
                    inside(s, e).start()

        @pl.when(t == 2 * beats)
        def _():
            for s in range(sections):
                for e in range(planes):
                    arrival(s, (partner + 2 * e) % n_row).wait_recv()

        @pl.when((d == 2) & (j < chunks))
        def _():
            multiply(col, j, True)

        def lagged(apart):
            for side in (1, -1):
                origin = z - side * apart

                @pl.when((apart < lines) & (origin >= 0) & (origin < lines))
                def _(origin=origin):
                    multiply(*place(origin, j))

        def crossed(apart):
            for side in (1, -1):
                origin = z - side * apart
                due = True if side > 0 else apart > 0
                due = due & (j < chunks) & ((apart == 0) | (j >= paired))

                @pl.when(due & (origin >= 0) & (origin < lines))
                def _(origin=origin):
                    for e in range(1, width):
                        there = (x + e) % width

                        @pl.when(j >= paired)
                        def _(e=e, there=there):
                            across(origin, j, e, there).wait_recv()

                        multiply(origin * width + there, j)

        def late(i, carry):
            lagged(i)
            crossed(i - 1)
            return carry

        lax.fori_loop(jnp.where(d == 2, 1, d), jnp.where(d < 2, d, d + 1), late, 0)
        return carry

    lax.fori_loop(0, (lines + 1) * beats, step, 0)

    def drain(t, carry):
        origin, j = t // beats, t % beats

        @pl.when((origin <= z) & (z < lines - 1))
        def _():
            along(origin, j, 1).wait_send()

        @pl.when((origin >= z) & (z > 0))
        def _():
            along(origin, j, -1).wait_send()

        @pl.when((j < chunks) & ((origin == z) | (j >= paired)))
        def _():
            for e in range(1, width):
                across(origin, j, e).wait_send()

        return carry

    lax.fori_loop(0, lines * beats, drain, 0)
    for s in range(sections):
        for e in range(1, planes):
            beside(s, e).wait_send()
        for e in range(planes):
            inside(s, e).wait_send()


def spread_multiply(amp_piece, integrals, factors, n_col, n_row, tile):
    lines = 4 if n_col % 4 == 0 else n_col
    width = n_col // lines
    rows, depth = amp_piece.shape
    sections, slab_rows, out_cols = integrals.shape
    planes = n_row // 2
    chunk = 384 if rows % 384 == 0 else rows
    chunks = rows // chunk
    beats = chunks + (chunks // 6 if width == 2 else 0)
    return pl.pallas_call(
        functools.partial(spread_kernel, lines, width, n_row, chunk, tile),
        out_shape=pltpu.VMEM((rows, out_cols), jnp.float32),
        in_specs=[
            pl.BlockSpec(memory_space=pl.ANY),
            pl.BlockSpec(memory_space=pltpu.VMEM),
            pl.BlockSpec(memory_space=pltpu.VMEM),
        ],
        out_specs=pl.BlockSpec(memory_space=pltpu.VMEM),
        scratch_shapes=[
            pltpu.VMEM((n_col, rows, depth), jnp.bfloat16),
            pltpu.VMEM((sections * n_row, slab_rows, out_cols), jnp.bfloat16),
            pltpu.SemaphoreType.DMA,
            pltpu.SemaphoreType.DMA((2, lines, beats)),
            pltpu.SemaphoreType.DMA((lines, beats)),
            pltpu.SemaphoreType.DMA((max(width - 1, 1), lines, chunks)),
            pltpu.SemaphoreType.DMA((n_col, chunks)),
            pltpu.SemaphoreType.DMA((max(planes - 1, 1), sections)),
            pltpu.SemaphoreType.DMA((planes, sections)),
            pltpu.SemaphoreType.DMA((sections * n_row,)),
        ],
        compiler_params=pltpu.CompilerParams(
            collective_id=0, has_side_effects=True, vmem_limit_bytes=44 * 1024 * 1024
        ),
        cost_estimate=pl.CostEstimate(
            flops=2 * rows * depth * n_col * out_cols, bytes_accessed=40_000_000, transcendentals=0
        ),
    )(amp_piece, integrals, factors)


def deal_kernel(
    n_row, n_col, tile, a_ref, pair_ref, place_ref, out_ref, found_ref, keep, asend, ysend, csend, recv
):
    col = lax.axis_index("col")
    row = lax.axis_index("row")
    planes = n_row // 2
    partner = row + 1 - 2 * (row % 2)
    _, _, own_rows, width = out_ref.shape

    barrier = pltpu.get_barrier_semaphore()
    for e in range(1, n_col):
        pl.semaphore_signal(
            barrier, inc=1, device_id={"col": (col + e) % n_col}, device_id_type=MESH
        )
    pl.semaphore_signal(barrier, inc=1, device_id={"row": partner}, device_id_type=MESH)
    for e in range(1, planes):
        pl.semaphore_signal(
            barrier, inc=1, device_id={"row": (row + 2 * e) % n_row}, device_id_type=MESH
        )
    pl.semaphore_wait(barrier, n_col + planes - 1)

    def cut(c):
        return a_ref.at[:, pl.ds(pl.multiple_of(c * width, width), width)]

    def dealt(e):
        to = (col + e) % n_col
        return pltpu.make_async_remote_copy(
            src_ref=cut(to),
            dst_ref=out_ref.at[row, col],
            send_sem=asend.at[e],
            recv_sem=recv.at[row, col],
            device_id={"col": to},
            device_id_type=MESH,
        )

    def sent(held, c, to, sem, src=None):
        return pltpu.make_async_remote_copy(
            src_ref=out_ref.at[held, c] if src is None else src,
            dst_ref=out_ref.at[held, c],
            send_sem=sem,
            recv_sem=recv.at[held, c],
            device_id={"row": to},
            device_id_type=MESH,
        )

    def beside(c, e, src=None):
        return sent(row, c, (row + 2 * e) % n_row, ysend.at[e - 1, c], src)

    def inside(c, e, src=None):
        return sent((row + 2 * e) % n_row, c, partner, csend.at[e, c], src)

    mine = pltpu.make_async_copy(cut(col), out_ref.at[row, col], keep)
    mine.start()
    for e in range(1, planes):
        beside(col, e, cut(col)).start()

    def start(e, carry):
        dealt(e).start()
        return carry

    lax.fori_loop(1, n_col, start, 0)
    inside(col, 0, cut(col)).start()

    total = pair_ref.shape[1]
    tiles = found_ref.shape[0]
    block = total // 8
    found_ref[...] = jnp.zeros_like(found_ref)

    def invert(i, carry):
        at = pl.ds(pl.multiple_of(i * block, block), block)
        pairs = pair_ref[:, at]
        here = lax.broadcasted_iota(jnp.int32, (tiles, block), 0) * tile + row * (tiles * tile)
        high = jnp.where((pairs >= here) & (pairs < here + tile), 1.0, 0.0).astype(jnp.bfloat16)
        low = (pairs & (tile - 1)) == lax.broadcasted_iota(jnp.int32, (tile, block), 0)
        for half in range(2):
            value = jnp.where(low, place_ref[half : half + 1, at], 0.0).astype(jnp.bfloat16)
            found_ref[:, half * tile : (half + 1) * tile] += lax.dot_general(
                high, value, (((1,), (1,)), ((), ())), preferred_element_type=jnp.float32
            )
        return carry

    lax.fori_loop(0, 8, invert, 0)

    def step(e, carry):
        @pl.when((e > 0) & (e < n_col))
        def _():
            c = (col + n_col - e) % n_col
            sent(row, c, partner, csend.at[0, c]).wait_recv()
            for f in range(1, planes):
                beside(c, f).start()
            inside(c, 0).start()

        @pl.when(e > 0)
        def _():
            c = (col + n_col - (e - 1)) % n_col
            for f in range(1, planes):
                sent((row + 2 * f) % n_row, c, partner, csend.at[f, c]).wait_recv()
                inside(c, f).start()

        return carry

    lax.fori_loop(0, n_col + 1, step, 0)
    mine.wait()

    def drain(c, carry):
        for f in range(planes):
            sent((partner + 2 * f) % n_row, c, partner, csend.at[f, c]).wait_recv()
            inside(c, f).wait_send()
        for f in range(1, planes):
            beside(c, f).wait_send()

        @pl.when(c > 0)
        def _():
            dealt(c).wait_send()

        return carry

    lax.fori_loop(0, n_col, drain, 0)


def deal(amp_owned, pairs, places, n_row, n_col, tile):
    own_rows, width_all = amp_owned.shape
    tiles = pairs.shape[1] // n_row // tile
    planes = n_row // 2
    return pl.pallas_call(
        functools.partial(deal_kernel, n_row, n_col, tile),
        out_shape=(
            pltpu.HBM((n_row, n_col, own_rows, width_all // n_col), jnp.bfloat16),
            jax.ShapeDtypeStruct((tiles, 2 * tile), jnp.float32),
        ),
        in_specs=[
            pl.BlockSpec(memory_space=pltpu.HBM),
            pl.BlockSpec(memory_space=pltpu.VMEM),
            pl.BlockSpec(memory_space=pltpu.VMEM),
        ],
        out_specs=(pl.BlockSpec(memory_space=pltpu.HBM), pl.BlockSpec(memory_space=pltpu.VMEM)),
        scratch_shapes=[
            pltpu.SemaphoreType.DMA,
            pltpu.SemaphoreType.DMA((n_col,)),
            pltpu.SemaphoreType.DMA((max(planes - 1, 1), n_col)),
            pltpu.SemaphoreType.DMA((planes, n_col)),
            pltpu.SemaphoreType.DMA((n_row, n_col)),
        ],
        compiler_params=pltpu.CompilerParams(
            collective_id=1, has_side_effects=True, vmem_limit_bytes=32 * 1024 * 1024
        ),
    )(amp_owned, pairs, places)


def on_device(amp_owned, pair_of_slot, amp_tiles, integrals, integral_tile_mask):
    n_col = lax.axis_size("col")
    n_row = lax.axis_size("row")
    col_at = lax.axis_index("col")
    row_at = lax.axis_index("row")
    own_rows, width_all = amp_owned.shape
    total_rows = pair_of_slot.shape[0]
    grid_rows = total_rows // n_row
    sections, slab_rows, out_cols = integrals.shape
    tile_size = total_rows // amp_tiles.shape[0]
    piece_cols = width_all // n_col
    row_tiles = grid_rows // tile_size
    piece_tiles = piece_cols // tile_size

    local_tile_rows = slab_rows // tile_size
    col_tiles = out_cols // tile_size
    tiles_int = lax.dynamic_slice(
        integral_tile_mask,
        (0, row_at * local_tile_rows, col_at * col_tiles),
        (sections, local_tile_rows, col_tiles),
    )
    factors = jnp.repeat(
        tiles_int.reshape(sections * local_tile_rows, col_tiles).astype(jnp.bfloat16), tile_size, axis=1
    )

    slot = jnp.arange(total_rows, dtype=jnp.int32)
    owner, within = slot // own_rows, slot % own_rows
    place = ((owner % n_row) * n_col + owner // n_row) * own_rows + within
    places = jnp.stack([place // 128, place % 128]).astype(jnp.float32)
    everyone, found = deal(amp_owned, pair_of_slot[None, :], places, n_row, n_col, tile_size)
    everyone = everyone.reshape(total_rows, piece_cols)
    found = found.astype(jnp.int32)
    found = (found[:, :tile_size] * 128 + found[:, tile_size:]).reshape(grid_rows)

    my_tiles = lax.dynamic_slice(
        amp_tiles, (row_at * row_tiles, col_at * piece_tiles), (row_tiles, piece_tiles)
    )
    amp_piece = apply_tile_blocks(
        everyone.at[found].get(mode="promise_in_bounds"), my_tiles, tile_size
    )
    return 0.5 * spread_multiply(amp_piece, integrals, factors, n_col, n_row, tile_size)


def solution(mesh):
    placed = (P(("col", "row"), None), P(), P(), P(None, "row", "col"), P())
    return jax.shard_map(
        on_device, mesh=mesh, in_specs=placed, out_specs=P("row", "col"), check_vma=False
    )
```
